128 devices in a mesh: node: 4 (over x), surf: 32 (over z, y, core).
Axes of the slice: x: 4, y: 4, z: 4, core: 2. Of those that a mesh axis runs over, the one named last changes fastest.
Arguments:
- sens: bfloat16 [256, 3, 524288], P('node', None, 'surf'), may hold values from -6 to 6
- psi: float32 [35, 256], replicated, may hold values from -4 to 4
- quad_table: float32 [16], replicated, may hold values from 0.004 to 0.04
- quad_index: int32 [256], replicated, may hold values from 0 to 15
- counts: int32 [1024], P('surf'), may hold values from 1 to 512, 327680 in all
- cells: int32 [1024], P('surf'), may hold values from 0 to 383, as said below
- coords: float32 [3, 524288], P(None, 'surf'), may hold values from 0 to 1
Outputs:
- gradient: float32 [105, 24576], P(None, ('node', 'surf'))
The draws below stay inside these ranges and needn't reach their ends.
Inputs may be any that keep to these rules, and one draw needn't show every extreme that they name: `counts`: some patch is full, with 512 live points, in every draw. `cells`: cell e belongs to owner e // 3. Within each aligned block of 8 patches, no two patches have the same owner.
All inputs are finite; a program needn't handle non-finite values. No bound on the sum of `counts` on one device may be relied on, other than what follows from the above.
Results may differ from the reference program's by a relative error of at most 0.003.
Values may be sent and summed in bfloat16 or wider, within the bound.
No kernel may reach another device: no remote copies, remote signals or barrier semaphores. Data moves between devices by JAX's collectives and lax.ppermute only.
A program may use at most 128 MiB of HBM per device.

```python
import math
import jax
import jax.numpy as jnp
import numpy as np
from jax import lax

Q = 256
K = 35
NQW = 16
CELLS = 384
PATCH_PTS = 512
PATCH_SURF = 32
PATCHES = 1024
POINTS = 524288
N_NODE = 4
N_SURF = 32
DEVICES = 128


def draw_cells(key, part):
    block_size = PATCH_SURF // N_NODE
    nblocks = PATCHES // block_size
    per_owner = CELLS // DEVICES
    owner_key = jax.random.fold_in(key, 11)
    local_key = jax.random.fold_in(key, 23)
    roll_key = jax.random.fold_in(key, 37)
    block_keys = jax.random.split(owner_key, nblocks)
    blocks = jnp.arange(nblocks, dtype=jnp.int32)
    handler = blocks % N_NODE * N_SURF + blocks // N_NODE
    target = (handler + DEVICES // 2) % DEVICES
    fixed_offset = DEVICES // 2 - 1
    rolls = jax.random.randint(roll_key, (nblocks,), 0, block_size).astype(jnp.int32)

    def one_block(one_key, aim, amount):
        values = jnp.arange(1, DEVICES - 1, dtype=jnp.int32)
        values = values + (values >= fixed_offset).astype(jnp.int32)
        rest = jax.random.permutation(one_key, values).astype(jnp.int32)
        head = jnp.array([0, fixed_offset], dtype=jnp.int32)
        offsets = jnp.concatenate([head, rest[:block_size - 2]])
        offsets = jnp.roll(offsets, amount)
        return (aim + offsets) % DEVICES
    owners = jax.vmap(one_block)(block_keys, target, rolls)
    owners = owners.reshape(-1).astype(jnp.int32)
    within = jax.random.randint(local_key, (PATCHES,), 0, per_owner).astype(jnp.int32)
    return owners * per_owner + within


def plant(drawn, stream_key, smallest, largest):
    place = [jax.random.randint(jax.random.fold_in(stream_key, axis), (), 0, length) for axis, length in enumerate(drawn.shape)]
    longest = drawn.shape.index(max(drawn.shape))
    beside = place[:longest] + [(place[longest] + 1) % drawn.shape[longest]] + place[longest + 1:]
    return drawn.at[tuple(place)].set(smallest).at[tuple(beside)].set(largest)


def shard_levels(stream_key, extent, cuts, low, top_value):
    level, own = 1.0, jax.random.fold_in(stream_key, 6)
    for axis_at, shards_of in cuts:
        steps = jnp.exp(jax.random.uniform(jax.random.fold_in(own, axis_at), (shards_of,), jnp.float32, low / len(cuts), top_value / len(cuts)))
        level = level * jnp.repeat(steps, extent[axis_at] // shards_of).reshape([-1 if axis == axis_at else 1 for axis in range(len(extent))])
    return level


def length_profile(number_of, total, bound, lean):
    portions = [(1 << 20) // math.isqrt(standing ** lean) + 1 for standing in range(2, number_of + 1)]
    surplus, holding = total - bound - (number_of - 1), [1] * (number_of - 1)
    while surplus > 0:
        free = [i for i in range(number_of - 1) if holding[i] < bound]
        whole, left = sum([portions[i] for i in free]), surplus
        for i in free:
            addition = min(bound - holding[i], max(1, left * portions[i] // whole), surplus)
            holding[i] = holding[i] + addition
            surplus = surplus - addition
    return np.array([bound] + holding)


def ragged_sizes(stream_key, count, total, most, lean):
    if count == 2:
        one = jax.random.randint(stream_key, (), max(1, total - most), min(most, total - 1) + 1)
        return jnp.stack([one, total - one])
    tallies = jnp.asarray(length_profile(count, total, most, lean), jnp.int32)
    twos = (count - 1) // 2
    giver, receiver = tallies[1:1 + 2 * twos:2], tallies[2:2 + 2 * twos:2]
    slack = jnp.minimum(giver - 1, most - receiver)
    passed = jax.random.randint(jax.random.fold_in(stream_key, 1), (twos,), 0, 1 << 20) % (slack + 1)
    tallies = tallies.at[1:1 + 2 * twos:2].set(giver - passed).at[2:2 + 2 * twos:2].set(receiver + passed)
    return tallies[jax.random.permutation(jax.random.fold_in(stream_key, 2), count)]


def scatter_about(rng, shape, scale, reach, shards=(), kind=jnp.bfloat16):
    drawn = scale * jax.random.normal(rng, shape, jnp.float32)
    if shards:
        drawn = drawn * shard_levels(rng, shape, shards, -0.22, 0.18)
    return jnp.clip(drawn, -reach, reach).astype(kind)


def setup_inputs(seed: int = 0) -> dict:
    keys = jax.random.split(jax.random.key(seed), 8)
    return {
        "sens": scatter_about(keys[0], (Q, 3, POINTS), 1.0, 6.0, ((0, 4), (2, 32))),
        "psi": scatter_about(keys[1], (K, Q), 1.0, 4.0, (), jnp.float32),
        "quad_table": jnp.clip(jnp.exp(jax.random.uniform(keys[2], (NQW,), jnp.float32, math.log(0.004), math.log(0.04))), 0.004, 0.04),
        "quad_index": plant(jax.random.randint(keys[3], (Q,), 0, NQW), jax.random.fold_in(keys[3], 1), 0, NQW - 1).astype(jnp.int32),
        "counts": ragged_sizes(keys[4], PATCHES, PATCHES * PATCH_PTS * 5 // 8, PATCH_PTS, 2).astype(jnp.int32),
        "cells": draw_cells(jax.random.fold_in(keys[7], 71), 0),
        "coords": jnp.clip(1.0 * jax.random.uniform(keys[6], (3, POINTS), jnp.float32) ** shard_levels(keys[6], (3, POINTS), ((1, 32),), -0.2, 0.2), 0.0, 1.0),
    }


def bernstein(coords, live):
    one = 1.0 - coords
    basis = jnp.stack([one * one * one, 3.0 * coords * one * one, 3.0 * coords * coords * one, coords * coords * coords], axis=1)
    weights = basis[0][:, None, None, :] * basis[1][None, :, None, :] * basis[2][None, None, :, :]
    return weights.reshape(64, -1) * live[None, :]


def lattice_part(chaos, counts, cells, coords):
    npatch = counts.shape[0]
    slots = jnp.arange(PATCH_PTS, dtype=jnp.int32)
    live = (slots[None, :] < counts[:, None]).astype(jnp.float32).reshape(-1)
    bern = bernstein(coords, live).reshape(64, npatch, PATCH_PTS)
    flat = chaos.reshape(3 * K, npatch, PATCH_PTS)
    tiles = jnp.einsum("apn,tpn->pat", flat, bern, precision=lax.Precision.HIGHEST)
    hits = (cells[:, None] == jnp.arange(CELLS, dtype=jnp.int32)[None, :]).astype(jnp.float32)
    spread = jnp.einsum("pe,pat->aet", hits, tiles, precision=lax.Precision.HIGHEST)
    return spread.reshape(3 * K, CELLS * 64)


def reference(sens, psi, quad_table, quad_index, counts, cells, coords):
    hits = (quad_index[:, None] == jnp.arange(NQW, dtype=jnp.int32)[None, :]).astype(jnp.float32)
    qweight = jnp.dot(hits, quad_table, precision=lax.Precision.HIGHEST)
    coef = (psi * qweight[None, :]).astype(jnp.bfloat16).astype(jnp.float32)
    npts = PATCH_SURF * PATCH_PTS

    def one_block(total, index):
        start = (index * npts).astype(jnp.int32)
        block = lax.dynamic_slice_in_dim(sens, start, npts, 2).astype(jnp.float32)
        chaos = jnp.einsum("kq,qcn->kcn", coef, block, precision=lax.Precision.HIGHEST)
        pstart = (index * PATCH_SURF).astype(jnp.int32)
        bcounts = lax.dynamic_slice_in_dim(counts, pstart, PATCH_SURF, 0)
        bcells = lax.dynamic_slice_in_dim(cells, pstart, PATCH_SURF, 0)
        bcoords = lax.dynamic_slice_in_dim(coords, start, npts, 1)
        return total + lattice_part(chaos, bcounts, bcells, bcoords), None

    start_total = jnp.zeros((3 * K, CELLS * 64), jnp.float32)
    total, unused = lax.scan(one_block, start_total, jnp.arange(N_SURF, dtype=jnp.int32))
    return total
```

```python
import jax
import jax.numpy as jnp
from jax import lax
from jax.experimental import pallas as pl
from jax.experimental.pallas import tpu as pltpu
from jax.sharding import Mesh, PartitionSpec as P

K = 35
NQW = 16
CELLS = 384
PATCH_PTS = 512
NODE_Q = 64
STEP_PATCHES = 4
ROWS = 56
LANES = 128
MIB = 1 << 20


def bernstein_rows(coords, count):
    shape = (8, PATCH_PTS)
    u, v, w = [jnp.broadcast_to(row, shape) for row in coords]
    sub = lax.broadcasted_iota(jnp.int32, shape, 0)
    lane = lax.broadcasted_iota(jnp.int32, shape, 1)
    live = (lane < count).astype(jnp.float32)

    def basis(a):
        one = 1.0 - a
        return one * one * one, 3.0 * a * one * one, 3.0 * a * a * one, a * a * a

    w0, w1, w2, w3 = basis(w)
    low = sub & 3
    wl = jnp.where(low == 0, w0, jnp.where(low == 1, w1, jnp.where(low == 2, w2, w3))) * live
    v0, v1, v2, v3 = basis(v)
    first = sub < 4
    pair01 = jnp.where(first, v0, v1) * wl
    pair23 = jnp.where(first, v2, v3) * wl
    rows = []
    for b in basis(u):
        rows += [b * pair01, b * pair23]
    return jnp.concatenate(rows, axis=0)


def split(x):
    high = x.astype(jnp.bfloat16)
    return high, (x - high.astype(jnp.float32)).astype(jnp.bfloat16)


def weights(table_ref, index_ref, psi_ref, pad_ref, w_ref):
    index = index_ref[...]
    qweight = jnp.zeros(index.shape, jnp.float32)
    for j in range(NQW):
        qweight = jnp.where(index == j, table_ref[j], qweight)
    pad_ref[...] = jnp.zeros_like(pad_ref)
    pad_ref[0:K, :] = psi_ref[...] * qweight
    coef = pad_ref[...].astype(jnp.bfloat16)
    node = lax.axis_index("x")
    row = lax.broadcasted_iota(jnp.int32, (112, 40), 0)
    col = lax.broadcasted_iota(jnp.int32, (112, 40), 1)
    expand = ((row - 3 * col >= 0) & (row - 3 * col < 3)).astype(jnp.float32).astype(jnp.bfloat16)
    spread = jnp.dot(expand, coef, preferred_element_type=jnp.float32).astype(jnp.bfloat16)
    q = lax.broadcasted_iota(jnp.int32, (256, 384), 0)
    col = lax.broadcasted_iota(jnp.int32, (256, 384), 1)
    pick = (q == node * NODE_Q + (col & 63)).astype(jnp.float32).astype(jnp.bfloat16)
    full = jnp.dot(spread, pick, preferred_element_type=jnp.float32)
    row = lax.broadcasted_iota(jnp.int32, (112, 384), 0)
    col = lax.broadcasted_iota(jnp.int32, (112, 384), 1)
    w_ref[...] = jnp.where(row % 3 == (col // 64) % 3, full, 0.0).astype(jnp.bfloat16)


def tiles_kernel(counts_ref, table_ref, index_ref, psi_ref, sens_ref, coords_ref, out_ref, pad_ref, w_ref):
    step = pl.program_id(0)

    @pl.when(step == 0)
    def _():
        weights(table_ref, index_ref, psi_ref, pad_ref, w_ref)

    lower = lax.broadcasted_iota(jnp.int32, (192, LANES), 1) < 64
    lower_slot = lower[:ROWS]
    w = w_ref[...]
    for pair in range(STEP_PATCHES // 2):
        both = []
        for half in range(2):
            i = 2 * pair + half
            at = slice(i * PATCH_PTS, (i + 1) * PATCH_PTS)
            count = counts_ref[step * STEP_PATCHES + i]
            bern = bernstein_rows([coords_ref[c : c + 1, at] for c in range(3)], count)
            high, low = split(bern)
            rhs = jnp.concatenate([high, low], axis=0)
            lhs = jnp.concatenate([sens_ref[c, :, at] for c in range(3)], axis=0)
            s = lax.dot_general(lhs, rhs, (((1,), (1,)), ((), ())), preferred_element_type=jnp.float32)
            both.append(s + pltpu.roll(s, 64, 1))
        high, low = split(jnp.where(lower, both[0], both[1]))
        t = jnp.dot(w, jnp.concatenate([high, low], axis=0), preferred_element_type=jnp.float32)
        top, bottom = t[0:ROWS], t[ROWS : 2 * ROWS]
        out_ref[2 * pair] = jnp.where(lower_slot, top, pltpu.roll(bottom, 64, 1)).astype(jnp.bfloat16)
        out_ref[2 * pair + 1] = jnp.where(lower_slot, pltpu.roll(top, 64, 1), bottom).astype(jnp.bfloat16)


def partial_tiles(sens, psi, quad_table, quad_index, counts, coords):
    npatch = counts.shape[0]
    points = STEP_PATCHES * PATCH_PTS
    smem = pl.BlockSpec(memory_space=pltpu.SMEM)
    return pl.pallas_call(
        tiles_kernel,
        grid=(npatch // STEP_PATCHES,),
        in_specs=[
            smem,
            smem,
            pl.BlockSpec((1, 256), lambda i: (0, 0)),
            pl.BlockSpec((K, 256), lambda i: (0, 0)),
            pl.BlockSpec((3, NODE_Q, points), lambda i: (0, 0, i)),
            pl.BlockSpec((3, points), lambda i: (0, i)),
        ],
        out_specs=pl.BlockSpec((STEP_PATCHES, ROWS, LANES), lambda i: (i, 0, 0)),
        out_shape=jax.ShapeDtypeStruct((npatch, ROWS, LANES), jnp.bfloat16),
        scratch_shapes=[pltpu.VMEM((40, 256), jnp.float32), pltpu.VMEM((112, 384), jnp.bfloat16)],
        compiler_params=pltpu.CompilerParams(vmem_limit_bytes=32 * MIB),
        name="tiles",
    )(counts, quad_table, quad_index.reshape(1, 256), psi, sens.transpose(1, 0, 2), coords)


def node_sum_kernel(cells_ref, in_ref, out_ref):
    row = lax.broadcasted_iota(jnp.int32, (ROWS, LANES), 0)
    lane = lax.broadcasted_iota(jnp.int32, (ROWS, LANES), 1)
    node = lax.axis_index("x")
    for p in range(8):
        total = in_ref[p].astype(jnp.float32)
        for j in range(1, 4):
            total = total + in_ref[8 * j + p].astype(jnp.float32)
        cell = cells_ref[8 * node + p]
        owner = cell // 3
        within = cell - 3 * owner
        mark = jnp.where(lane < 96, owner, within).astype(jnp.float32)
        out_ref[p] = jnp.where((row == ROWS - 1) & (lane >= 64), mark, total).astype(jnp.bfloat16)


def node_sum(parts, cells):
    return pl.pallas_call(
        node_sum_kernel,
        in_specs=[pl.BlockSpec(memory_space=pltpu.SMEM), pl.BlockSpec(memory_space=pltpu.VMEM)],
        out_specs=pl.BlockSpec(memory_space=pltpu.VMEM),
        out_shape=jax.ShapeDtypeStruct((8, ROWS, LANES), jnp.bfloat16),
        compiler_params=pltpu.CompilerParams(vmem_limit_bytes=16 * MIB),
        name="node_sum",
    )(cells, parts)


def combine_kernel(in_ref, out_ref, acc_ref, mark_ref, scalar_ref, sem):
    count = in_ref.shape[0]
    acc_ref[...] = jnp.zeros_like(acc_ref)
    for p in range(count):
        mark_ref[p : p + 1, :] = in_ref[p].astype(jnp.float32)[ROWS - 1 : ROWS, :].astype(jnp.int32)
    copy = pltpu.make_async_copy(mark_ref, scalar_ref, sem)
    copy.start()
    copy.wait()
    my_y, my_core = lax.axis_index("y"), lax.axis_index("core")

    def body(p, carry):
        owner, within = scalar_ref[p, 64], scalar_ref[p, 96]
        surf = owner & 31
        mine = (((surf >> 1) & 3) == my_y) & ((surf & 1) == my_core)

        @pl.when(mine)
        def _():
            at = ((owner >> 5) * 4 + (surf >> 3)) * 3 + within
            acc_ref[at] += in_ref[p].astype(jnp.float32)

        return carry

    lax.fori_loop(0, count, body, 0)
    out_ref[...] = acc_ref[...].astype(jnp.bfloat16)


def combine(tiles):
    count = tiles.shape[0]
    return pl.pallas_call(
        combine_kernel,
        in_specs=[pl.BlockSpec(memory_space=pltpu.VMEM)],
        out_specs=pl.BlockSpec(memory_space=pltpu.VMEM),
        out_shape=jax.ShapeDtypeStruct((48, ROWS, LANES), jnp.bfloat16),
        scratch_shapes=[
            pltpu.VMEM((48, ROWS, LANES), jnp.float32),
            pltpu.VMEM((count, LANES), jnp.int32),
            pltpu.SMEM((count, LANES), jnp.int32),
            pltpu.SemaphoreType.DMA,
        ],
        compiler_params=pltpu.CompilerParams(vmem_limit_bytes=16 * MIB),
        name="combine",
    )(tiles)


def owner_sum_kernel(in_ref, out_ref):
    lower = lax.broadcasted_iota(jnp.int32, (ROWS, LANES), 1) < 64
    cell = []
    for e in range(3):
        total = in_ref[e].astype(jnp.float32)
        for j in range(1, in_ref.shape[0] // 3):
            total = total + in_ref[3 * j + e].astype(jnp.float32)
        cell.append(total)
    a, b, c = cell
    rest = 3 * K - ROWS
    out_ref[0:ROWS, 0:128] = jnp.where(lower, a, pltpu.roll(b, 64, 1))
    out_ref[0:ROWS, 128:192] = c[:, 0:64]
    out_ref[ROWS : 3 * K, 0:128] = jnp.where(lower, pltpu.roll(a, 64, 1), b)[0:rest]
    out_ref[ROWS : 3 * K, 128:192] = pltpu.roll(c, 64, 1)[0:rest, 0:64]


def owner_sum(slots):
    return pl.pallas_call(
        owner_sum_kernel,
        in_specs=[pl.BlockSpec(memory_space=pltpu.VMEM)],
        out_specs=pl.BlockSpec(memory_space=pltpu.VMEM),
        out_shape=jax.ShapeDtypeStruct((3 * K, 192), jnp.float32),
        compiler_params=pltpu.CompilerParams(vmem_limit_bytes=16 * MIB),
        name="owner_sum",
    )(slots)


def local(sens, psi, quad_table, quad_index, counts, cells, coords):
    parts = partial_tiles(sens, psi, quad_table, quad_index, counts, coords)
    parts = lax.all_to_all(parts, "x", 0, 0, tiled=True)
    tiles = node_sum(parts, cells)
    tiles = lax.all_gather(tiles, ("y", "core"), axis=0, tiled=True)
    slots = combine(tiles)
    slots = lax.all_to_all(slots, ("x", "z"), 0, 0, tiled=True)
    return owner_sum(slots)


def solution(mesh):
    inner = Mesh(mesh.devices.reshape(4, 4, 4, 2), ("x", "z", "y", "core"))
    surf = ("z", "y", "core")
    in_specs = (P("x", None, surf), P(), P(), P(), P(surf), P(surf), P(None, surf))
    out_specs = P(None, ("x",) + surf)
    return jax.shard_map(local, mesh=inner, in_specs=in_specs, out_specs=out_specs, check_vma=False)
```

```python
import jax
import jax.numpy as jnp
from jax import lax
from jax.experimental import pallas as pl
from jax.experimental.pallas import tpu as pltpu
from jax.sharding import Mesh, PartitionSpec as P

K = 35
NQW = 16
CELLS = 384
PATCH_PTS = 512
NODE_Q = 64
STEP_PATCHES = 4
HALF = 16
ROWS = 56
LANES = 128
MIB = 1 << 20
KERNEL_VMEM = 57 * MIB


def bernstein_rows(coords, count):
    shape = (8, PATCH_PTS)
    u, v, w = [jnp.broadcast_to(row, shape) for row in coords]
    sub = lax.broadcasted_iota(jnp.int32, shape, 0)
    lane = lax.broadcasted_iota(jnp.int32, shape, 1)
    live = (lane < count).astype(jnp.float32)

    def basis(a):
        one = 1.0 - a
        return one * one * one, 3.0 * a * one * one, 3.0 * a * a * one, a * a * a

    w0, w1, w2, w3 = basis(w)
    low = sub & 3
    wl = jnp.where(low == 0, w0, jnp.where(low == 1, w1, jnp.where(low == 2, w2, w3))) * live
    v0, v1, v2, v3 = basis(v)
    first = sub < 4
    pair01 = jnp.where(first, v0, v1) * wl
    pair23 = jnp.where(first, v2, v3) * wl
    rows = []
    for b in basis(u):
        rows += [b * pair01, b * pair23]
    return jnp.concatenate(rows, axis=0)


def split(x):
    high = x.astype(jnp.bfloat16)
    return high, (x - high.astype(jnp.float32)).astype(jnp.bfloat16)


def weights(table_ref, index_ref, psi_ref, pad_ref, w_ref):
    index = index_ref[...]
    qweight = jnp.zeros(index.shape, jnp.float32)
    for j in range(NQW):
        qweight = jnp.where(index == j, table_ref[j], qweight)
    pad_ref[...] = jnp.zeros_like(pad_ref)
    pad_ref[0:K, :] = psi_ref[...] * qweight
    coef = pad_ref[...].astype(jnp.bfloat16)
    node = lax.axis_index("x")
    row = lax.broadcasted_iota(jnp.int32, (112, 40), 0)
    col = lax.broadcasted_iota(jnp.int32, (112, 40), 1)
    expand = ((row - 3 * col >= 0) & (row - 3 * col < 3)).astype(jnp.float32).astype(jnp.bfloat16)
    spread = jnp.dot(expand, coef, preferred_element_type=jnp.float32).astype(jnp.bfloat16)
    q = lax.broadcasted_iota(jnp.int32, (256, 384), 0)
    col = lax.broadcasted_iota(jnp.int32, (256, 384), 1)
    pick = (q == node * NODE_Q + (col & 63)).astype(jnp.float32).astype(jnp.bfloat16)
    full = jnp.dot(spread, pick, preferred_element_type=jnp.float32)
    row = lax.broadcasted_iota(jnp.int32, (112, 384), 0)
    col = lax.broadcasted_iota(jnp.int32, (112, 384), 1)
    w_ref[...] = jnp.where(row % 3 == (col // 64) % 3, full, 0.0).astype(jnp.bfloat16)


def tiles_of(half, step, counts_ref, sens_ref, coords_ref, w_ref, keep_ref, send_ref):
    lower = lax.broadcasted_iota(jnp.int32, (192, LANES), 1) < 64
    lower_slot = lower[:ROWS]
    w = w_ref[...]
    for pair in range(STEP_PATCHES // 2):
        both = []
        for i in (2 * pair, 2 * pair + 1):
            at = slice(i * PATCH_PTS, (i + 1) * PATCH_PTS)
            count = counts_ref[half * HALF + step * STEP_PATCHES + i]
            bern = bernstein_rows([coords_ref[c : c + 1, at] for c in range(3)], count)
            high, low = split(bern)
            rhs = jnp.concatenate([high, low], axis=0)
            lhs = jnp.concatenate([sens_ref[c, :, at] for c in range(3)], axis=0)
            s = lax.dot_general(lhs, rhs, (((1,), (1,)), ((), ())), preferred_element_type=jnp.float32)
            both.append(s + pltpu.roll(s, 64, 1))
        high, low = split(jnp.where(lower, both[0], both[1]))
        t = jnp.dot(w, jnp.concatenate([high, low], axis=0), preferred_element_type=jnp.float32)
        top, bottom = t[0:ROWS], t[ROWS : 2 * ROWS]
        first = jnp.where(lower_slot, top, pltpu.roll(bottom, 64, 1))
        second = jnp.where(lower_slot, pltpu.roll(top, 64, 1), bottom)
        for i, x in ((2 * pair, first), (2 * pair + 1, second)):
            keep_ref[STEP_PATCHES * step + i] = x
            send_ref[STEP_PATCHES * step + i] = x.astype(jnp.bfloat16)


HALF_STEPS = HALF // STEP_PATCHES
SMEM = pl.BlockSpec(memory_space=pltpu.SMEM)
VMEM = pl.BlockSpec(memory_space=pltpu.VMEM)
HBM = pl.BlockSpec(memory_space=pltpu.HBM)


def stream_copies(half, step, sens_ref, coords_ref, sens_buf, coords_buf, sem):
    points = STEP_PATCHES * PATCH_PTS
    at = pl.ds(pl.multiple_of((half * HALF_STEPS + step) * points, points), points)
    return (
        pltpu.make_async_copy(sens_ref.at[:, :, at], sens_buf.at[step], sem.at[step, 0]),
        pltpu.make_async_copy(coords_ref.at[:, at], coords_buf.at[step], sem.at[step, 1]),
    )


def half_tiles(half, counts_ref, sens_ref, coords_ref, w_ref, keep_hbm, send_hbm, sens_buf, coords_buf, sem, keep_ref, send_ref, out_sem):
    def out_copies(step):
        at = pl.ds(step * STEP_PATCHES, STEP_PATCHES)
        return (
            pltpu.make_async_copy(send_ref.at[at], send_hbm.at[at], out_sem.at[step, 0]),
            pltpu.make_async_copy(keep_ref.at[at], keep_hbm.at[at], out_sem.at[step, 1]),
        )

    def body(step, carry):
        for copy in stream_copies(half, step, sens_ref, coords_ref, sens_buf, coords_buf, sem):
            copy.wait()
        tiles_of(half, step, counts_ref, sens_buf.at[step], coords_buf.at[step], w_ref, keep_ref, send_ref)
        for copy in out_copies(step):
            copy.start()
        return carry

    lax.fori_loop(0, HALF_STEPS, body, 0)
    for step in range(HALF_STEPS):
        for copy in out_copies(step):
            copy.wait()


def start_stream(half, sens_ref, coords_ref, sens_buf, coords_buf, sem):
    for step in range(HALF_STEPS):
        for copy in stream_copies(half, step, sens_ref, coords_ref, sens_buf, coords_buf, sem):
            copy.start()


def first_kernel(
    counts_hbm, table_hbm, index_hbm, psi_hbm, sens_ref, coords_ref, w_hbm, keep_hbm, send_hbm,
    sens_buf, coords_buf, sem, keep_ref, send_ref, out_sem, counts_ref, w_ref, w_sem,
    table_ref, index_ref, psi_ref, small_sem, pad_ref
):
    pairs = ((table_hbm, table_ref), (index_hbm, index_ref), (psi_hbm, psi_ref), (counts_hbm, counts_ref))
    small = [pltpu.make_async_copy(a, b, small_sem.at[i]) for i, (a, b) in enumerate(pairs)]
    for copy in small:
        copy.start()
    start_stream(0, sens_ref, coords_ref, sens_buf, coords_buf, sem)
    for copy in small:
        copy.wait()
    weights(table_ref, index_ref, psi_ref, pad_ref, w_ref)
    w_copy = pltpu.make_async_copy(w_ref, w_hbm, w_sem)
    w_copy.start()
    bufs = (sens_buf, coords_buf, sem, keep_ref, send_ref, out_sem)
    half_tiles(0, counts_ref, sens_ref, coords_ref, w_ref, keep_hbm, send_hbm, *bufs)
    w_copy.wait()


def second_kernel(
    counts_hbm, w_hbm, sens_ref, coords_ref, keep_hbm, send_hbm,
    sens_buf, coords_buf, sem, keep_ref, send_ref, out_sem, counts_ref, w_ref, w_sem, small_sem
):
    small = [pltpu.make_async_copy(counts_hbm, counts_ref, small_sem), pltpu.make_async_copy(w_hbm, w_ref, w_sem)]
    for copy in small:
        copy.start()
    start_stream(1, sens_ref, coords_ref, sens_buf, coords_buf, sem)
    for copy in small:
        copy.wait()
    bufs = (sens_buf, coords_buf, sem, keep_ref, send_ref, out_sem)
    half_tiles(1, counts_ref, sens_ref, coords_ref, w_ref, keep_hbm, send_hbm, *bufs)


def partial_tiles(half, counts, first, second, sens, coords):
    points = STEP_PATCHES * PATCH_PTS
    tiles = [jax.ShapeDtypeStruct((HALF, ROWS, LANES), t) for t in (jnp.float32, jnp.bfloat16)]
    scratch = [
        pltpu.VMEM((HALF_STEPS, 3, NODE_Q, points), jnp.bfloat16),
        pltpu.VMEM((HALF_STEPS, 3, points), jnp.float32),
        pltpu.SemaphoreType.DMA((HALF_STEPS, 2)),
        pltpu.VMEM((HALF, ROWS, LANES), jnp.float32),
        pltpu.VMEM((HALF, ROWS, LANES), jnp.bfloat16),
        pltpu.SemaphoreType.DMA((HALF_STEPS, 2)),
        pltpu.SMEM(counts.shape, jnp.int32),
        pltpu.VMEM((112, 384), jnp.bfloat16),
        pltpu.SemaphoreType.DMA,
    ]
    kinds = dict(
        compiler_params=pltpu.CompilerParams(vmem_limit_bytes=KERNEL_VMEM),
        cost_estimate=pl.CostEstimate(flops=int(8e9), bytes_accessed=int(4e6), transcendentals=0),
    )
    if half == 0:
        table, index = first
        return pl.pallas_call(
            first_kernel,
            in_specs=[HBM] * 6,
            out_specs=[HBM] * 3,
            out_shape=[jax.ShapeDtypeStruct((112, 384), jnp.bfloat16)] + tiles,
            scratch_shapes=scratch
            + [
                pltpu.SMEM((NQW,), jnp.float32),
                pltpu.VMEM((1, 256), jnp.int32),
                pltpu.VMEM((K, 256), jnp.float32),
                pltpu.SemaphoreType.DMA((4,)),
                pltpu.VMEM((40, 256), jnp.float32),
            ],
            name="tiles_first",
            **kinds,
        )(counts, table, index.reshape(1, 256), second, sens, coords)
    return pl.pallas_call(
        second_kernel,
        in_specs=[HBM] * 4,
        out_specs=[HBM] * 2,
        out_shape=tiles,
        scratch_shapes=scratch + [pltpu.SemaphoreType.DMA],
        name="tiles_second",
        **kinds,
    )(counts, first, sens, coords)


def small_call(kernel, out_shape, in_specs, args, name, scratch=()):
    many = isinstance(out_shape, list)
    return pl.pallas_call(
        kernel,
        in_specs=in_specs,
        out_specs=[VMEM] * len(out_shape) if many else VMEM,
        out_shape=out_shape,
        scratch_shapes=list(scratch),
        compiler_params=pltpu.CompilerParams(vmem_limit_bytes=16 * MIB),
        name=name,
    )(*args)


def pair_sum_kernel(keep_ref, recv_ref, after_ref, sum_ref, send_ref):
    del after_ref
    total = keep_ref[...] + recv_ref[...].astype(jnp.float32)
    sum_ref[...] = total
    send_ref[...] = total.astype(jnp.bfloat16)


def pair_sum(keep, recv, after):
    out = [jax.ShapeDtypeStruct(keep.shape, t) for t in (jnp.float32, jnp.bfloat16)]
    in_specs = [VMEM, VMEM, pl.BlockSpec(memory_space=pl.ANY)]
    return small_call(pair_sum_kernel, out, in_specs, (keep, recv, after), "pair_sum")


def add_mine(cells_ref, dense_ref, count, tile):
    my_x, my_core = lax.axis_index("x"), lax.axis_index("core")

    def body(p, carry):
        cell = cells_ref[p]
        owner = cell // 3
        within = cell - 3 * owner

        @pl.when(((owner >> 5) == my_x) & ((owner & 1) == my_core))
        def _():
            at = ((owner & 31) >> 1) * 3 + within
            dense_ref[at] += tile(p)

        return carry

    lax.fori_loop(0, count, body, 0)


def own_kernel(cells_ref, a_ref, b_ref, dense_ref):
    dense_ref[...] = jnp.zeros_like(dense_ref)
    add_mine(cells_ref, dense_ref, HALF, lambda p: a_ref[p])
    add_mine(cells_ref.at[pl.ds(HALF, HALF)], dense_ref, HALF, lambda p: b_ref[p])


def other_kernel(cells_ref, dense_ref, a_ref, b_ref, out_ref, acc_ref):
    acc_ref[...] = dense_ref[...]
    add_mine(cells_ref, acc_ref, HALF, lambda p: a_ref[p].astype(jnp.float32))
    add_mine(cells_ref.at[pl.ds(HALF, HALF)], acc_ref, HALF, lambda p: b_ref[p].astype(jnp.float32))
    out_ref[...] = acc_ref[...].astype(jnp.bfloat16)


def owner_sum_kernel(in_ref, out_ref):
    lower = lax.broadcasted_iota(jnp.int32, (ROWS, LANES), 1) < 64
    cell = []
    for e in range(3):
        total = in_ref[e].astype(jnp.float32)
        for j in range(1, in_ref.shape[0] // 3):
            total = total + in_ref[3 * j + e].astype(jnp.float32)
        cell.append(total)
    a, b, c = cell
    ab = jnp.concatenate([jnp.where(lower, a, pltpu.roll(b, 64, 1)), jnp.where(lower, pltpu.roll(a, 64, 1), b)], axis=0)
    cc = jnp.concatenate([c, pltpu.roll(c, 64, 1)], axis=0)
    out_ref[0:128, :] = ab.T[:, 0 : 3 * K]
    out_ref[128:192, :] = cc.T[0:64, 0 : 3 * K]


def double(step):
    near, far = (1, 0, 3, 2), (3, 2, 1, 0)
    order = (near, far) if step == 0 else (far, near)
    return [(2 * x + core, 2 * order[core][x] + core) for x in range(4) for core in range(2)]


def local(sens, psi, quad_table, quad_index, counts, cells, coords):
    swap = [(0, 1), (1, 0)]
    other_cells = lax.ppermute(cells, "core", swap)
    sens = sens.transpose(1, 0, 2)
    w, keep_a, send_a = partial_tiles(0, counts, (quad_table, quad_index), psi, sens, coords)
    recv_a = lax.ppermute(send_a, ("x", "core"), double(0))
    keep_b, send_b = partial_tiles(1, counts, w, None, sens, coords)
    recv_b = lax.ppermute(send_b, ("x", "core"), double(0))
    keep_a, send_a = pair_sum(keep_a, recv_a, w)
    recv_a = lax.ppermute(send_a, ("x", "core"), double(1))
    keep_b, send_b = pair_sum(keep_b, recv_b, send_a)
    recv_b = lax.ppermute(send_b, ("x", "core"), double(1))
    full_a, send_a = pair_sum(keep_a, recv_a, send_b)
    recv_a = lax.ppermute(send_a, "core", swap)
    full_b, send_b = pair_sum(keep_b, recv_b, send_a)
    recv_b = lax.ppermute(send_b, "core", swap)
    slot = (48, ROWS, LANES)
    dense = small_call(own_kernel, jax.ShapeDtypeStruct(slot, jnp.float32), [SMEM, VMEM, VMEM], (cells, full_a, full_b), "own")
    out = jax.ShapeDtypeStruct(slot, jnp.bfloat16)
    args = (other_cells, dense, recv_a, recv_b)
    slots = small_call(other_kernel, out, [SMEM] + [VMEM] * 3, args, "other", [pltpu.VMEM(slot, jnp.float32)])
    slots = lax.all_to_all(slots, ("z", "y"), 0, 0, tiled=True)
    out = jax.ShapeDtypeStruct((192, 3 * K), jnp.float32)
    return small_call(owner_sum_kernel, out, [VMEM], (slots,), "owner_sum").T


def solution(mesh):
    inner = Mesh(mesh.devices.reshape(4, 4, 4, 2), ("x", "z", "y", "core"))
    surf = ("z", "y", "core")
    in_specs = (P("x", None, surf), P(), P(), P(), P(surf), P(surf), P(None, surf))
    out_specs = P(None, ("x",) + surf)
    return jax.shard_map(local, mesh=inner, in_specs=in_specs, out_specs=out_specs, check_vma=False)
```

```python
import functools

import jax
import jax.numpy as jnp
from jax import lax
from jax.experimental import pallas as pl
from jax.experimental.pallas import tpu as pltpu
from jax.sharding import Mesh, PartitionSpec as P

K = 35
NQW = 16
CELLS = 384
PATCH_PTS = 512
NODE_Q = 64
PART = 16
CHUNK = 8
ROWS = 56
LANES = 128
MIB = 1 << 20
KERNEL_VMEM = 32 * MIB


def bernstein_rows(coords, count):
    shape = (8, PATCH_PTS)
    u, v, w = [jnp.broadcast_to(row, shape) for row in coords]
    sub = lax.broadcasted_iota(jnp.int32, shape, 0)
    lane = lax.broadcasted_iota(jnp.int32, shape, 1)
    live = (lane < count).astype(jnp.float32)

    def basis(a):
        one = 1.0 - a
        return one * one * one, 3.0 * a * one * one, 3.0 * a * a * one, a * a * a

    w0, w1, w2, w3 = basis(w)
    low = sub & 3
    wl = jnp.where(low == 0, w0, jnp.where(low == 1, w1, jnp.where(low == 2, w2, w3))) * live
    v0, v1, v2, v3 = basis(v)
    first = sub < 4
    pair01 = jnp.where(first, v0, v1) * wl
    pair23 = jnp.where(first, v2, v3) * wl
    rows = []
    for b in basis(u):
        rows += [b * pair01, b * pair23]
    return jnp.concatenate(rows, axis=0)


def split(x):
    high = x.astype(jnp.bfloat16)
    return high, (x - high.astype(jnp.float32)).astype(jnp.bfloat16)


SMEM = pl.BlockSpec(memory_space=pltpu.SMEM)
VMEM = pl.BlockSpec(memory_space=pltpu.VMEM)
HBM = pl.BlockSpec(memory_space=pltpu.HBM)
CHUNKS = PART // CHUNK
POINTS = CHUNK * PATCH_PTS


def weights(table_ref, index_ref, psi_ref, pad_ref, w_ref):
    index = index_ref[...]
    qweight = jnp.zeros(index.shape, jnp.float32)
    for j in range(NQW):
        qweight = jnp.where(index == j, table_ref[j], qweight)
    pad_ref[...] = jnp.zeros_like(pad_ref)
    pad_ref[0:K, :] = psi_ref[...] * qweight
    coef = pad_ref[...].astype(jnp.bfloat16)
    node = lax.axis_index("x")
    row = lax.broadcasted_iota(jnp.int32, (112, 40), 0)
    col = lax.broadcasted_iota(jnp.int32, (112, 40), 1)
    expand = ((row - 3 * col >= 0) & (row - 3 * col < 3)).astype(jnp.float32).astype(jnp.bfloat16)
    spread = jnp.dot(expand, coef, preferred_element_type=jnp.float32).astype(jnp.bfloat16)
    q = lax.broadcasted_iota(jnp.int32, (256, 192), 0)
    col = lax.broadcasted_iota(jnp.int32, (256, 192), 1)
    pick = (q == node * NODE_Q + (col & 63)).astype(jnp.float32).astype(jnp.bfloat16)
    full = jnp.dot(spread, pick, preferred_element_type=jnp.float32)
    row = lax.broadcasted_iota(jnp.int32, (112, 192), 0)
    col = lax.broadcasted_iota(jnp.int32, (112, 192), 1)
    w_ref[...] = jnp.where(row % 3 == col // 64, full, 0.0).astype(jnp.bfloat16)


def across(a, b):
    return lax.dot_general(a, b, (((1,), (1,)), ((), ())), preferred_element_type=jnp.float32)


def chunk_tiles(chunk, counts, sens_ref, coords_ref, w, keep_ref, send_ref):
    lower = lax.broadcasted_iota(jnp.int32, (ROWS, LANES), 1) < 64
    for pair in range(CHUNK // 2):
        sums = []
        for i in (2 * pair, 2 * pair + 1):
            at = slice(i * PATCH_PTS, (i + 1) * PATCH_PTS)
            bern = bernstein_rows([coords_ref[chunk, c : c + 1, at] for c in range(3)], counts(chunk * CHUNK + i))
            basis = jnp.concatenate(split(bern), axis=0)
            s = across(basis, sens_ref[chunk, :, :, at].reshape(3 * NODE_Q, PATCH_PTS))
            sums.append(s[0:64] + s[64:128])
        high, low = split(jnp.concatenate(sums, axis=0))
        t = across(w, high) + across(w, low)
        top, bottom = t[0:ROWS], t[ROWS : 2 * ROWS]
        first = jnp.where(lower, top, pltpu.roll(bottom, 64, 1))
        second = jnp.where(lower, pltpu.roll(top, 64, 1), bottom)
        for i, x in ((2 * pair, first), (2 * pair + 1, second)):
            keep_ref[chunk * CHUNK + i] = x
            send_ref[chunk * CHUNK + i] = x.astype(jnp.bfloat16)


def part_copies(part, chunk, sens_hbm, coords_hbm, sens_buf, coords_buf, sem):
    at = pl.ds((part * CHUNKS + chunk) * POINTS, POINTS)
    return (
        pltpu.make_async_copy(sens_hbm.at[:, :, at], sens_buf.at[chunk], sem.at[chunk, 0]),
        pltpu.make_async_copy(coords_hbm.at[:, at], coords_buf.at[chunk], sem.at[chunk, 1]),
    )


def first_kernel(
    counts_hbm, table_hbm, index_hbm, psi_hbm, sens_hbm, coords_hbm,
    keep_ref, send_ref, w_ref, count_rows, sens_next, coords_next,
    sens_buf, coords_buf, sem, next_sem, counts_ref, table_ref, index_ref, psi_ref, small_sem, pad_ref
):
    pairs = ((table_hbm, table_ref), (index_hbm, index_ref), (psi_hbm, psi_ref), (counts_hbm, counts_ref))
    small = [pltpu.make_async_copy(a, b, small_sem.at[i]) for i, (a, b) in enumerate(pairs)]
    mine = [part_copies(0, chunk, sens_hbm, coords_hbm, sens_buf, coords_buf, sem) for chunk in range(CHUNKS)]
    later = [part_copies(1, chunk, sens_hbm, coords_hbm, sens_next, coords_next, next_sem) for chunk in range(CHUNKS)]
    for copy in [*mine[0], *small] + [c for pair in mine[1:] for c in pair]:
        copy.start()
    for copy in small:
        copy.wait()
    for p in range(count_rows.shape[0]):
        count_rows[p : p + 1, :] = jnp.full((1, LANES), counts_ref[p], jnp.int32)
    weights(table_ref, index_ref, psi_ref, pad_ref, w_ref)
    w = w_ref[...]
    for chunk in range(CHUNKS):
        for copy in mine[chunk]:
            copy.wait()
        for copy in later[chunk]:
            copy.start()
        chunk_tiles(chunk, lambda p: counts_ref[p], sens_buf, coords_buf, w, keep_ref, send_ref)
    for pair in later:
        for copy in pair:
            copy.wait()


def later_kernel(part, last, count_rows, w_ref, sens_buf, coords_buf, *rest):
    if last:
        keep_ref, send_ref = rest
        later = []
    else:
        sens_hbm, coords_hbm, keep_ref, send_ref, sens_next, coords_next, next_sem = rest
        later = [
            part_copies(part + 1, chunk, sens_hbm, coords_hbm, sens_next, coords_next, next_sem)
            for chunk in range(CHUNKS)
        ]
    for pair in later:
        for copy in pair:
            copy.start()
    w = w_ref[...]

    def counts(p):
        row = count_rows[part * PART + p : part * PART + p + 1, :]
        return jnp.concatenate([row] * (PATCH_PTS // LANES), axis=1)

    for chunk in range(CHUNKS):
        chunk_tiles(chunk, counts, sens_buf, coords_buf, w, keep_ref, send_ref)
    for pair in later:
        for copy in pair:
            copy.wait()


def kinds():
    return dict(
        compiler_params=pltpu.CompilerParams(vmem_limit_bytes=KERNEL_VMEM),
        cost_estimate=pl.CostEstimate(flops=int(8e9), bytes_accessed=int(4e6), transcendentals=0),
    )


TILES = [jax.ShapeDtypeStruct((PART, ROWS, LANES), t) for t in (jnp.float32, jnp.bfloat16)]
BUFFERS = ((CHUNKS, 3, NODE_Q, POINTS), jnp.bfloat16), ((CHUNKS, 3, POINTS), jnp.float32)
STREAM = [jax.ShapeDtypeStruct(*b) for b in BUFFERS]


def first_part(counts, table, index, psi, sens, coords):
    return pl.pallas_call(
        first_kernel,
        in_specs=[HBM] * 6,
        out_specs=[VMEM] * 6,
        out_shape=TILES
        + [jax.ShapeDtypeStruct((112, 192), jnp.bfloat16), jax.ShapeDtypeStruct((counts.shape[0], LANES), jnp.int32)]
        + STREAM,
        scratch_shapes=[pltpu.VMEM(*b) for b in BUFFERS]
        + [
            pltpu.SemaphoreType.DMA((CHUNKS, 2)),
            pltpu.SemaphoreType.DMA((CHUNKS, 2)),
            pltpu.SMEM(counts.shape, jnp.int32),
            pltpu.SMEM((NQW,), jnp.float32),
            pltpu.VMEM((1, 256), jnp.int32),
            pltpu.VMEM((K, 256), jnp.float32),
            pltpu.SemaphoreType.DMA((4,)),
            pltpu.VMEM((40, 256), jnp.float32),
        ],
        name="tiles_0",
        **kinds(),
    )(counts, table, index, psi, sens, coords)


def later_part(part, count_rows, w, stream, sens, coords):
    last = (part + 1) * PART * PATCH_PTS == sens.shape[2]
    return pl.pallas_call(
        functools.partial(later_kernel, part, last),
        in_specs=[VMEM] * 4 + ([] if last else [HBM] * 2),
        out_specs=[VMEM] * (2 if last else 4),
        out_shape=TILES + ([] if last else STREAM),
        scratch_shapes=[] if last else [pltpu.SemaphoreType.DMA((CHUNKS, 2))],
        name="tiles_%d" % part,
        **kinds(),
    )(count_rows, w, *stream, *([] if last else [sens, coords]))


def all_parts(sens, psi, quad_table, quad_index, counts, coords):
    def hbm(x):
        return pltpu.with_memory_space_constraint(x, pltpu.HBM)

    sens, coords = hbm(sens.transpose(1, 0, 2)), hbm(coords)
    small = hbm(counts), hbm(quad_table), hbm(quad_index.reshape(1, 256)), hbm(psi)
    keep, send, w, count_rows, *stream = first_part(*small, sens, coords)
    yield keep, send, w
    for part in range(1, counts.shape[0] // PART):
        keep, send, *stream = later_part(part, count_rows, w, stream, sens, coords)
        yield keep, send, w


def small_call(kernel, out_shape, in_specs, args, name, scratch=()):
    many = isinstance(out_shape, list)
    return pl.pallas_call(
        kernel,
        in_specs=in_specs,
        out_specs=[VMEM] * len(out_shape) if many else VMEM,
        out_shape=out_shape,
        scratch_shapes=list(scratch),
        compiler_params=pltpu.CompilerParams(vmem_limit_bytes=16 * MIB),
        name=name,
    )(*args)


def pair_sum_kernel(keep_ref, recv_ref, after_ref, sum_ref, send_ref):
    del after_ref
    total = keep_ref[...] + recv_ref[...].astype(jnp.float32)
    sum_ref[...] = total
    send_ref[...] = total.astype(jnp.bfloat16)


def pair_sum(keep, recv, after):
    out = [jax.ShapeDtypeStruct(keep.shape, t) for t in (jnp.float32, jnp.bfloat16)]
    in_specs = [VMEM, VMEM, pl.BlockSpec(memory_space=pl.ANY)]
    return small_call(pair_sum_kernel, out, in_specs, (keep, recv, after), "pair_sum")


def add_mine(cells_ref, start, dense_ref, tiles_ref):
    my_x, my_core = lax.axis_index("x"), lax.axis_index("core")
    for p in range(PART):
        cell = cells_ref[start + p]
        owner = lax.shift_right_logical(cell * 43691, 17)
        within = cell - 3 * owner

        @pl.when(((owner >> 5) == my_x) & ((owner & 1) == my_core))
        def _():
            at = ((owner & 31) >> 1) * 3 + within
            dense_ref[at] += tiles_ref[p].astype(jnp.float32)


def own_kernel(cells_ref, *refs):
    *parts, dense_ref = refs
    dense_ref[...] = jnp.zeros_like(dense_ref)
    for i, part in enumerate(parts):
        add_mine(cells_ref, i * PART, dense_ref, part)


def other_kernel(cells_ref, in_ref, *refs):
    *parts, out_ref, dense_ref = refs
    dense_ref[...] = in_ref[...]
    for i, part in enumerate(parts):
        add_mine(cells_ref, i * PART, dense_ref, part)
    out_ref[...] = dense_ref[...].astype(jnp.bfloat16)


def owner_sum_kernel(in_ref, out_ref):
    lower = lax.broadcasted_iota(jnp.int32, (ROWS, LANES), 1) < 64
    cell = []
    for e in range(3):
        total = in_ref[e].astype(jnp.float32)
        for j in range(1, in_ref.shape[0] // 3):
            total = total + in_ref[3 * j + e].astype(jnp.float32)
        cell.append(total)
    a, b, c = cell
    ab = jnp.concatenate([jnp.where(lower, a, pltpu.roll(b, 64, 1)), jnp.where(lower, pltpu.roll(a, 64, 1), b)], axis=0)
    cc = jnp.concatenate([c, pltpu.roll(c, 64, 1)], axis=0)
    out_ref[0:128, :] = ab.T[:, 0 : 3 * K]
    out_ref[128:192, :] = cc.T[0:64, 0 : 3 * K]


def double(step):
    near, far = (1, 0, 3, 2), (3, 2, 1, 0)
    order = (near, far) if step == 0 else (far, near)
    return [(2 * x + core, 2 * order[core][x] + core) for x in range(4) for core in range(2)]


def local(sens, psi, quad_table, quad_index, counts, cells, coords):
    swap = [(0, 1), (1, 0)]

    def smem(x):
        return pltpu.with_memory_space_constraint(x, pltpu.SMEM)

    other_cells = lax.ppermute(cells, "core", swap)
    held = []
    for keep, send, w in all_parts(sens, psi, quad_table, quad_index, counts, coords):
        held.append((keep, lax.ppermute(send, ("x", "core"), double(0))))
    after = w
    for i, (keep, recv) in enumerate(held):
        keep, after = pair_sum(keep, recv, after)
        held[i] = keep, lax.ppermute(after, ("x", "core"), double(1))
    for i, (keep, recv) in enumerate(held):
        full, after = pair_sum(keep, recv, after)
        held[i] = full, lax.ppermute(after, "core", swap)
    full, swapped = zip(*held)
    slot = (48, ROWS, LANES)
    specs = [VMEM] * len(full)
    dense = jax.ShapeDtypeStruct(slot, jnp.float32)
    dense = small_call(own_kernel, dense, [SMEM] + specs, (smem(cells), *full), "own")
    slots = jax.ShapeDtypeStruct(slot, jnp.bfloat16)
    args = (smem(other_cells), dense, *swapped)
    slots = small_call(other_kernel, slots, [SMEM, VMEM] + specs, args, "other", [pltpu.VMEM(slot, jnp.float32)])
    slots = lax.all_to_all(slots, ("z", "y"), 0, 0, tiled=True)
    out = jax.ShapeDtypeStruct((192, 3 * K), jnp.float32)
    return small_call(owner_sum_kernel, out, [VMEM], (slots,), "owner_sum").T


def solution(mesh):
    inner = Mesh(mesh.devices.reshape(4, 4, 4, 2), ("x", "z", "y", "core"))
    surf = ("z", "y", "core")
    in_specs = (P("x", None, surf), P(), P(), P(), P(surf), P(surf), P(None, surf))
    out_specs = P(None, ("x",) + surf)
    return jax.shard_map(local, mesh=inner, in_specs=in_specs, out_specs=out_specs, check_vma=False)
```

```python
import functools

import jax
import jax.numpy as jnp
from jax import lax
from jax.experimental import pallas as pl
from jax.experimental.pallas import tpu as pltpu
from jax.sharding import Mesh, PartitionSpec as P

K = 35
NQW = 16
CELLS = 384
PATCH_PTS = 512
NODE_Q = 64
PART = 16
FIRST_CHUNKS = (4, 12)
NEXT_CHUNKS = (16,)
ROWS = 56
LANES = 128
MIB = 1 << 20
KERNEL_VMEM = 32 * MIB


def bernstein_rows(coords, count):
    shape = (8, PATCH_PTS)
    u, v, w = [jnp.broadcast_to(row, shape) for row in coords]
    sub = lax.broadcasted_iota(jnp.int32, shape, 0)
    lane = lax.broadcasted_iota(jnp.int32, shape, 1)
    live = (lane < count).astype(jnp.float32)

    def basis(a):
        one = 1.0 - a
        return one * one * one, 3.0 * a * one * one, 3.0 * a * a * one, a * a * a

    w0, w1, w2, w3 = basis(w)
    low = sub & 3
    wl = jnp.where(low == 0, w0, jnp.where(low == 1, w1, jnp.where(low == 2, w2, w3))) * live
    v0, v1, v2, v3 = basis(v)
    first = sub < 4
    pair01 = jnp.where(first, v0, v1) * wl
    pair23 = jnp.where(first, v2, v3) * wl
    rows = []
    for b in basis(u):
        rows += [b * pair01, b * pair23]
    return jnp.concatenate(rows, axis=0)


def split(x):
    high = x.astype(jnp.bfloat16)
    return high, (x - high.astype(jnp.float32)).astype(jnp.bfloat16)


SMEM = pl.BlockSpec(memory_space=pltpu.SMEM)
VMEM = pl.BlockSpec(memory_space=pltpu.VMEM)
HBM = pl.BlockSpec(memory_space=pltpu.HBM)


def weights(table_ref, index_ref, psi_ref, pad_ref, w_ref):
    index = index_ref[...]
    qweight = jnp.zeros(index.shape, jnp.float32)
    for j in range(NQW):
        qweight = jnp.where(index == j, table_ref[j], qweight)
    pad_ref[...] = jnp.zeros_like(pad_ref)
    pad_ref[0:K, :] = psi_ref[...] * qweight
    coef = pad_ref[...].astype(jnp.bfloat16)
    node = lax.axis_index("x")
    row = lax.broadcasted_iota(jnp.int32, (112, 40), 0)
    col = lax.broadcasted_iota(jnp.int32, (112, 40), 1)
    expand = ((row - 3 * col >= 0) & (row - 3 * col < 3)).astype(jnp.float32).astype(jnp.bfloat16)
    spread = jnp.dot(expand, coef, preferred_element_type=jnp.float32).astype(jnp.bfloat16)
    q = lax.broadcasted_iota(jnp.int32, (256, 192), 0)
    col = lax.broadcasted_iota(jnp.int32, (256, 192), 1)
    pick = (q == node * NODE_Q + (col & 63)).astype(jnp.float32).astype(jnp.bfloat16)
    full = jnp.dot(spread, pick, preferred_element_type=jnp.float32)
    row = lax.broadcasted_iota(jnp.int32, (112, 192), 0)
    col = lax.broadcasted_iota(jnp.int32, (112, 192), 1)
    w_ref[...] = jnp.where(row % 3 == col // 64, full, 0.0).astype(jnp.bfloat16)


def across(a, b):
    return lax.dot_general(a, b, (((1,), (1,)), ((), ())), preferred_element_type=jnp.float32)


def chunk_tiles(patches, counts, sens_ref, coords_ref, w, keep_ref, send_ref):
    lower = lax.broadcasted_iota(jnp.int32, (ROWS, LANES), 1) < 64
    for pair in range(patches.start, patches.stop, 2):
        sums = []
        for i in (pair, pair + 1):
            at = slice(i * PATCH_PTS, (i + 1) * PATCH_PTS)
            bern = bernstein_rows([coords_ref[c : c + 1, at] for c in range(3)], counts(i))
            basis = jnp.concatenate(split(bern), axis=0)
            s = across(basis, sens_ref[:, :, at].reshape(3 * NODE_Q, PATCH_PTS))
            sums.append(s[0:64] + s[64:128])
        high, low = split(jnp.concatenate(sums, axis=0))
        t = across(w, high) + across(w, low)
        top, bottom = t[0:ROWS], t[ROWS : 2 * ROWS]
        first = jnp.where(lower, top, pltpu.roll(bottom, 64, 1))
        second = jnp.where(lower, pltpu.roll(top, 64, 1), bottom)
        for i, x in ((pair, first), (pair + 1, second)):
            keep_ref[i] = x
            send_ref[i] = x.astype(jnp.bfloat16)


def chunks_of(sizes):
    ends = [sum(sizes[: i + 1]) for i in range(len(sizes))]
    return [range(end - size, end) for end, size in zip(ends, sizes)]


def part_copies(part, sizes, sens_hbm, coords_hbm, sens_buf, coords_buf, sem):
    copies = []
    for i, patches in enumerate(chunks_of(sizes)):
        count = len(patches) * PATCH_PTS
        here = pl.ds(patches.start * PATCH_PTS, count)
        there = pl.ds((part * PART + patches.start) * PATCH_PTS, count)
        copies.append(
            (
                pltpu.make_async_copy(sens_hbm.at[:, :, there], sens_buf.at[:, :, here], sem.at[i, 0]),
                pltpu.make_async_copy(coords_hbm.at[:, there], coords_buf.at[:, here], sem.at[i, 1]),
            )
        )
    return copies


def first_kernel(
    counts_hbm, table_hbm, index_hbm, psi_hbm, sens_hbm, coords_hbm,
    keep_ref, send_ref, w_ref, count_rows, sens_next, coords_next,
    sens_buf, coords_buf, sem, next_sem, counts_ref, table_ref, index_ref, psi_ref, small_sem, pad_ref
):
    pairs = ((table_hbm, table_ref), (index_hbm, index_ref), (psi_hbm, psi_ref), (counts_hbm, counts_ref))
    small = [pltpu.make_async_copy(a, b, small_sem.at[i]) for i, (a, b) in enumerate(pairs)]
    mine = part_copies(0, FIRST_CHUNKS, sens_hbm, coords_hbm, sens_buf, coords_buf, sem)
    later = part_copies(1, NEXT_CHUNKS, sens_hbm, coords_hbm, sens_next, coords_next, next_sem)
    for copy in [*mine[0], *small] + [c for pair in mine[1:] for c in pair]:
        copy.start()
    for copy in small:
        copy.wait()
    for p in range(count_rows.shape[0]):
        count_rows[p : p + 1, :] = jnp.full((1, LANES), counts_ref[p], jnp.int32)
    weights(table_ref, index_ref, psi_ref, pad_ref, w_ref)
    w = w_ref[...]
    for i, patches in enumerate(chunks_of(FIRST_CHUNKS)):
        for copy in mine[i]:
            copy.wait()
        for copy in later[i] if i < len(later) else ():
            copy.start()
        chunk_tiles(patches, lambda p: counts_ref[p], sens_buf, coords_buf, w, keep_ref, send_ref)
    for pair in later:
        for copy in pair:
            copy.wait()


def later_kernel(part, last, count_rows, w_ref, sens_buf, coords_buf, *rest):
    if last:
        keep_ref, send_ref = rest
        later = []
    else:
        sens_hbm, coords_hbm, keep_ref, send_ref, sens_next, coords_next, next_sem = rest
        later = part_copies(part + 1, NEXT_CHUNKS, sens_hbm, coords_hbm, sens_next, coords_next, next_sem)
    for pair in later:
        for copy in pair:
            copy.start()
    w = w_ref[...]

    def counts(p):
        row = count_rows[part * PART + p : part * PART + p + 1, :]
        return jnp.concatenate([row] * (PATCH_PTS // LANES), axis=1)

    chunk_tiles(range(PART), counts, sens_buf, coords_buf, w, keep_ref, send_ref)
    for pair in later:
        for copy in pair:
            copy.wait()


def kinds():
    return dict(
        compiler_params=pltpu.CompilerParams(vmem_limit_bytes=KERNEL_VMEM),
        cost_estimate=pl.CostEstimate(flops=int(8e9), bytes_accessed=int(4e6), transcendentals=0),
    )


TILES = [jax.ShapeDtypeStruct((PART, ROWS, LANES), t) for t in (jnp.float32, jnp.bfloat16)]
BUFFERS = ((3, NODE_Q, PART * PATCH_PTS), jnp.bfloat16), ((3, PART * PATCH_PTS), jnp.float32)
STREAM = [jax.ShapeDtypeStruct(*b) for b in BUFFERS]


def first_part(counts, table, index, psi, sens, coords):
    return pl.pallas_call(
        first_kernel,
        in_specs=[HBM] * 6,
        out_specs=[VMEM] * 6,
        out_shape=TILES
        + [jax.ShapeDtypeStruct((112, 192), jnp.bfloat16), jax.ShapeDtypeStruct((counts.shape[0], LANES), jnp.int32)]
        + STREAM,
        scratch_shapes=[pltpu.VMEM(*b) for b in BUFFERS]
        + [
            pltpu.SemaphoreType.DMA((len(FIRST_CHUNKS), 2)),
            pltpu.SemaphoreType.DMA((len(NEXT_CHUNKS), 2)),
            pltpu.SMEM(counts.shape, jnp.int32),
            pltpu.SMEM((NQW,), jnp.float32),
            pltpu.VMEM((1, 256), jnp.int32),
            pltpu.VMEM((K, 256), jnp.float32),
            pltpu.SemaphoreType.DMA((4,)),
            pltpu.VMEM((40, 256), jnp.float32),
        ],
        name="tiles_0",
        **kinds(),
    )(counts, table, index, psi, sens, coords)


def later_part(part, count_rows, w, stream, sens, coords):
    last = (part + 1) * PART * PATCH_PTS == sens.shape[2]
    return pl.pallas_call(
        functools.partial(later_kernel, part, last),
        in_specs=[VMEM] * 4 + ([] if last else [HBM] * 2),
        out_specs=[VMEM] * (2 if last else 4),
        out_shape=TILES + ([] if last else STREAM),
        scratch_shapes=[] if last else [pltpu.SemaphoreType.DMA((len(NEXT_CHUNKS), 2))],
        name="tiles_%d" % part,
        **kinds(),
    )(count_rows, w, *stream, *([] if last else [sens, coords]))


def all_parts(sens, psi, quad_table, quad_index, counts, coords):
    def hbm(x):
        return pltpu.with_memory_space_constraint(x, pltpu.HBM)

    sens, coords = hbm(sens.transpose(1, 0, 2)), hbm(coords)
    small = hbm(counts), hbm(quad_table), hbm(quad_index.reshape(1, 256)), hbm(psi)
    keep, send, w, count_rows, *stream = first_part(*small, sens, coords)
    yield keep, send, w
    for part in range(1, counts.shape[0] // PART):
        keep, send, *stream = later_part(part, count_rows, w, stream, sens, coords)
        yield keep, send, w


def small_call(kernel, out_shape, in_specs, args, name, aliases=None):
    many = isinstance(out_shape, list)
    return pl.pallas_call(
        kernel,
        in_specs=in_specs,
        out_specs=[VMEM] * len(out_shape) if many else VMEM,
        out_shape=out_shape,
        input_output_aliases=aliases or {},
        cost_estimate=pl.CostEstimate(flops=1, bytes_accessed=1, transcendentals=0),
        compiler_params=pltpu.CompilerParams(vmem_limit_bytes=16 * MIB),
        name=name,
    )(*args)


def pair_sum_kernel(keep_ref, recv_ref, after_ref, sum_ref, send_ref):
    del after_ref
    total = keep_ref[...] + recv_ref[...].astype(jnp.float32)
    sum_ref[...] = total
    send_ref[...] = total.astype(jnp.bfloat16)


def pair_sum(keep, recv, after):
    out = [jax.ShapeDtypeStruct(keep.shape, t) for t in (jnp.float32, jnp.bfloat16)]
    in_specs = [VMEM, VMEM, pl.BlockSpec(memory_space=pl.ANY)]
    return small_call(pair_sum_kernel, out, in_specs, (keep, recv, after), "pair_sum")


def add_mine(cells_ref, start, dense_ref, tiles_ref):
    my_x, my_core = lax.axis_index("x"), lax.axis_index("core")
    for p in range(PART):
        cell = cells_ref[start + p]
        owner = lax.shift_right_logical(cell * 43691, 17)
        within = cell - 3 * owner

        @pl.when(((owner >> 5) == my_x) & ((owner & 1) == my_core))
        def _():
            at = ((owner & 31) >> 1) * 3 + within
            dense_ref[at] += tiles_ref[p].astype(jnp.float32)


SLOTS = (48, ROWS, LANES)
DENSE = jax.ShapeDtypeStruct(SLOTS, jnp.float32)


def first_add_kernel(start, cells_ref, tiles_ref, dense_ref):
    dense_ref[...] = jnp.zeros_like(dense_ref)
    add_mine(cells_ref, start, dense_ref, tiles_ref)


def add_kernel(start, cells_ref, tiles_ref, in_ref, dense_ref):
    del in_ref
    add_mine(cells_ref, start, dense_ref, tiles_ref)


def last_add_kernel(start, cells_ref, tiles_ref, in_ref, dense_ref, out_ref):
    add_kernel(start, cells_ref, tiles_ref, in_ref, dense_ref)
    out_ref[...] = dense_ref[...].astype(jnp.bfloat16)


def add(cells, part, tiles, dense, last):
    start = part * PART
    if dense is None:
        kernel = functools.partial(first_add_kernel, start)
        return small_call(kernel, DENSE, [SMEM, VMEM], (cells, tiles), "first_add")
    args, specs = (cells, tiles, dense), [SMEM, VMEM, VMEM]
    if not last:
        return small_call(functools.partial(add_kernel, start), DENSE, specs, args, "add", {2: 0})
    out = [DENSE, jax.ShapeDtypeStruct(SLOTS, jnp.bfloat16)]
    return small_call(functools.partial(last_add_kernel, start), out, specs, args, "last_add", {2: 0})[1]


def owner_sum_kernel(in_ref, out_ref):
    lower = lax.broadcasted_iota(jnp.int32, (ROWS, LANES), 1) < 64
    cell = []
    for e in range(3):
        total = in_ref[e].astype(jnp.float32)
        for j in range(1, in_ref.shape[0] // 3):
            total = total + in_ref[3 * j + e].astype(jnp.float32)
        cell.append(total)
    a, b, c = cell
    ab = jnp.concatenate([jnp.where(lower, a, pltpu.roll(b, 64, 1)), jnp.where(lower, pltpu.roll(a, 64, 1), b)], axis=0)
    cc = jnp.concatenate([c, pltpu.roll(c, 64, 1)], axis=0)
    out_ref[0:128, :] = ab.T[:, 0 : 3 * K]
    out_ref[128:192, :] = cc.T[0:64, 0 : 3 * K]


def double(step):
    near, far = (1, 0, 3, 2), (3, 2, 1, 0)
    order = (near, far) if step == 0 else (far, near)
    return [(2 * x + core, 2 * order[core][x] + core) for x in range(4) for core in range(2)]


def local(sens, psi, quad_table, quad_index, counts, cells, coords):
    swap = [(0, 1), (1, 0)]

    def smem(x):
        return pltpu.with_memory_space_constraint(x, pltpu.SMEM)

    other_cells = lax.ppermute(cells, "core", swap)
    held = []
    for keep, send, w in all_parts(sens, psi, quad_table, quad_index, counts, coords):
        held.append((keep, lax.ppermute(send, ("x", "core"), double(0))))
    after = w
    for i, (keep, recv) in enumerate(held):
        keep, after = pair_sum(keep, recv, after)
        held[i] = keep, lax.ppermute(after, ("x", "core"), double(1))
    cells, other_cells = smem(cells), smem(other_cells)
    dense = None
    for i, (keep, recv) in enumerate(held):
        full, send = pair_sum(keep, recv, after)
        held[i] = lax.ppermute(send, "core", swap)
        after = dense = add(cells, i, full, dense, False)
    for i, swapped in enumerate(held):
        dense = add(other_cells, i, swapped, dense, i == len(held) - 1)
    slots = dense
    slots = lax.all_to_all(slots, ("z", "y"), 0, 0, tiled=True)
    out = jax.ShapeDtypeStruct((192, 3 * K), jnp.float32)
    return small_call(owner_sum_kernel, out, [VMEM], (slots,), "owner_sum").T


def solution(mesh):
    inner = Mesh(mesh.devices.reshape(4, 4, 4, 2), ("x", "z", "y", "core"))
    surf = ("z", "y", "core")
    in_specs = (P("x", None, surf), P(), P(), P(), P(surf), P(surf), P(None, surf))
    out_specs = P(None, ("x",) + surf)
    return jax.shard_map(local, mesh=inner, in_specs=in_specs, out_specs=out_specs, check_vma=False)
```

```python
import functools

import jax
import jax.numpy as jnp
from jax import lax
from jax.experimental import pallas as pl
from jax.experimental.pallas import tpu as pltpu
from jax.sharding import Mesh, PartitionSpec as P

K = 35
NQW = 16
CELLS = 384
PATCH_PTS = 512
NODE_Q = 64
PART = 16
FIRST_CHUNKS = (4, 12)
NEXT_CHUNKS = (16,)
ROWS = 56
LANES = 128
MIB = 1 << 20
KERNEL_VMEM = 32 * MIB


def bernstein_rows(coords, count):
    shape = (8, PATCH_PTS)
    u, v, w = [jnp.broadcast_to(row, shape) for row in coords]
    sub = lax.broadcasted_iota(jnp.int32, shape, 0)
    lane = lax.broadcasted_iota(jnp.int32, shape, 1)
    live = (lane < count).astype(jnp.float32)

    def basis(a):
        one = 1.0 - a
        return one * one * one, 3.0 * a * one * one, 3.0 * a * a * one, a * a * a

    w0, w1, w2, w3 = basis(w)
    low = sub & 3
    wl = jnp.where(low == 0, w0, jnp.where(low == 1, w1, jnp.where(low == 2, w2, w3))) * live
    v0, v1, v2, v3 = basis(v)
    first = sub < 4
    pair01 = jnp.where(first, v0, v1) * wl
    pair23 = jnp.where(first, v2, v3) * wl
    rows = []
    for b in basis(u):
        rows += [b * pair01, b * pair23]
    return jnp.concatenate(rows, axis=0)


def split(x):
    high = x.astype(jnp.bfloat16)
    return high, (x - high.astype(jnp.float32)).astype(jnp.bfloat16)


SMEM = pl.BlockSpec(memory_space=pltpu.SMEM)
VMEM = pl.BlockSpec(memory_space=pltpu.VMEM)
HBM = pl.BlockSpec(memory_space=pltpu.HBM)


def weights(table_ref, index_ref, psi_ref, pad_ref, w_ref):
    index = index_ref[...]
    qweight = jnp.zeros(index.shape, jnp.float32)
    for j in range(NQW):
        qweight = jnp.where(index == j, table_ref[j], qweight)
    pad_ref[...] = jnp.zeros_like(pad_ref)
    pad_ref[0:K, :] = psi_ref[...] * qweight
    coef = pad_ref[...].astype(jnp.bfloat16)
    node = lax.axis_index("x")
    row = lax.broadcasted_iota(jnp.int32, (112, 40), 0)
    col = lax.broadcasted_iota(jnp.int32, (112, 40), 1)
    expand = ((row - 3 * col >= 0) & (row - 3 * col < 3)).astype(jnp.float32).astype(jnp.bfloat16)
    spread = jnp.dot(expand, coef, preferred_element_type=jnp.float32).astype(jnp.bfloat16)
    q = lax.broadcasted_iota(jnp.int32, (256, 192), 0)
    col = lax.broadcasted_iota(jnp.int32, (256, 192), 1)
    pick = (q == node * NODE_Q + (col & 63)).astype(jnp.float32).astype(jnp.bfloat16)
    full = jnp.dot(spread, pick, preferred_element_type=jnp.float32)
    row = lax.broadcasted_iota(jnp.int32, (112, 192), 0)
    col = lax.broadcasted_iota(jnp.int32, (112, 192), 1)
    w_ref[...] = jnp.where(row % 3 == col // 64, full, 0.0).astype(jnp.bfloat16)


def across(a, b):
    return lax.dot_general(a, b, (((1,), (1,)), ((), ())), preferred_element_type=jnp.float32)


def chunk_tiles(patches, counts, sens_ref, coords_ref, w, keep_ref, send_ref):
    lower = lax.broadcasted_iota(jnp.int32, (ROWS, LANES), 1) < 64
    for pair in range(patches.start, patches.stop, 2):
        sums = []
        for i in (pair, pair + 1):
            at = slice(i * PATCH_PTS, (i + 1) * PATCH_PTS)
            bern = bernstein_rows([coords_ref[c : c + 1, at] for c in range(3)], counts(i))
            basis = jnp.concatenate(split(bern), axis=0)
            s = across(basis, sens_ref[:, :, at].reshape(3 * NODE_Q, PATCH_PTS))
            sums.append(s[0:64] + s[64:128])
        high, low = split(jnp.concatenate(sums, axis=0))
        t = across(w, high) + across(w, low)
        top, bottom = t[0:ROWS], t[ROWS : 2 * ROWS]
        first = jnp.where(lower, top, pltpu.roll(bottom, 64, 1))
        second = jnp.where(lower, pltpu.roll(top, 64, 1), bottom)
        for i, x in ((pair, first), (pair + 1, second)):
            keep_ref[i] = x
            send_ref[i] = x.astype(jnp.bfloat16)


def chunks_of(sizes):
    ends = [sum(sizes[: i + 1]) for i in range(len(sizes))]
    return [range(end - size, end) for end, size in zip(ends, sizes)]


def part_copies(part, sizes, sens_hbm, coords_hbm, sens_buf, coords_buf, sem):
    copies = []
    for i, patches in enumerate(chunks_of(sizes)):
        count = len(patches) * PATCH_PTS
        here = pl.ds(patches.start * PATCH_PTS, count)
        there = pl.ds((part * PART + patches.start) * PATCH_PTS, count)
        copies.append(
            (
                pltpu.make_async_copy(sens_hbm.at[:, :, there], sens_buf.at[:, :, here], sem.at[i, 0]),
                pltpu.make_async_copy(coords_hbm.at[:, there], coords_buf.at[:, here], sem.at[i, 1]),
            )
        )
    return copies


def first_kernel(
    counts_hbm, table_hbm, index_hbm, psi_hbm, sens_hbm, coords_hbm,
    keep_ref, send_ref, w_ref, count_rows, sens_next, coords_next,
    sens_buf, coords_buf, sem, next_sem, counts_ref, table_ref, index_ref, psi_ref, small_sem, pad_ref
):
    pairs = ((table_hbm, table_ref), (index_hbm, index_ref), (psi_hbm, psi_ref), (counts_hbm, counts_ref))
    small = [pltpu.make_async_copy(a, b, small_sem.at[i]) for i, (a, b) in enumerate(pairs)]
    mine = part_copies(0, FIRST_CHUNKS, sens_hbm, coords_hbm, sens_buf, coords_buf, sem)
    later = part_copies(1, NEXT_CHUNKS, sens_hbm, coords_hbm, sens_next, coords_next, next_sem)
    for copy in [*mine[0], *small] + [c for pair in mine[1:] for c in pair]:
        copy.start()
    for copy in small:
        copy.wait()
    for p in range(count_rows.shape[0]):
        count_rows[p : p + 1, :] = jnp.full((1, LANES), counts_ref[p], jnp.int32)
    weights(table_ref, index_ref, psi_ref, pad_ref, w_ref)
    w = w_ref[...]
    for i, patches in enumerate(chunks_of(FIRST_CHUNKS)):
        for copy in mine[i]:
            copy.wait()
        for copy in later[i] if i < len(later) else ():
            copy.start()
        chunk_tiles(patches, lambda p: counts_ref[p], sens_buf, coords_buf, w, keep_ref, send_ref)
    for pair in later:
        for copy in pair:
            copy.wait()


def later_kernel(part, last, count_rows, w_ref, sens_buf, coords_buf, *rest):
    if last:
        keep_ref, send_ref = rest
        later = []
    else:
        sens_hbm, coords_hbm, keep_ref, send_ref, sens_next, coords_next, next_sem = rest
        later = part_copies(part + 1, NEXT_CHUNKS, sens_hbm, coords_hbm, sens_next, coords_next, next_sem)
    for pair in later:
        for copy in pair:
            copy.start()
    w = w_ref[...]

    def counts(p):
        row = count_rows[part * PART + p : part * PART + p + 1, :]
        return jnp.concatenate([row] * (PATCH_PTS // LANES), axis=1)

    chunk_tiles(range(PART), counts, sens_buf, coords_buf, w, keep_ref, send_ref)
    for pair in later:
        for copy in pair:
            copy.wait()


def kinds():
    return dict(
        compiler_params=pltpu.CompilerParams(vmem_limit_bytes=KERNEL_VMEM),
        cost_estimate=pl.CostEstimate(flops=int(8e9), bytes_accessed=int(4e6), transcendentals=0),
    )


TILES = [jax.ShapeDtypeStruct((PART, ROWS, LANES), t) for t in (jnp.float32, jnp.bfloat16)]
BUFFERS = ((3, NODE_Q, PART * PATCH_PTS), jnp.bfloat16), ((3, PART * PATCH_PTS), jnp.float32)
STREAM = [jax.ShapeDtypeStruct(*b) for b in BUFFERS]


def first_part(counts, table, index, psi, sens, coords):
    return pl.pallas_call(
        first_kernel,
        in_specs=[HBM] * 6,
        out_specs=[VMEM] * 6,
        out_shape=TILES
        + [jax.ShapeDtypeStruct((112, 192), jnp.bfloat16), jax.ShapeDtypeStruct((counts.shape[0], LANES), jnp.int32)]
        + STREAM,
        scratch_shapes=[pltpu.VMEM(*b) for b in BUFFERS]
        + [
            pltpu.SemaphoreType.DMA((len(FIRST_CHUNKS), 2)),
            pltpu.SemaphoreType.DMA((len(NEXT_CHUNKS), 2)),
            pltpu.SMEM(counts.shape, jnp.int32),
            pltpu.SMEM((NQW,), jnp.float32),
            pltpu.VMEM((1, 256), jnp.int32),
            pltpu.VMEM((K, 256), jnp.float32),
            pltpu.SemaphoreType.DMA((4,)),
            pltpu.VMEM((40, 256), jnp.float32),
        ],
        name="tiles_0",
        **kinds(),
    )(counts, table, index, psi, sens, coords)


def later_part(part, count_rows, w, stream, sens, coords):
    last = (part + 1) * PART * PATCH_PTS == sens.shape[2]
    return pl.pallas_call(
        functools.partial(later_kernel, part, last),
        in_specs=[VMEM] * 4 + ([] if last else [HBM] * 2),
        out_specs=[VMEM] * (2 if last else 4),
        out_shape=TILES + ([] if last else STREAM),
        scratch_shapes=[] if last else [pltpu.SemaphoreType.DMA((len(NEXT_CHUNKS), 2))],
        name="tiles_%d" % part,
        **kinds(),
    )(count_rows, w, *stream, *([] if last else [sens, coords]))


def all_parts(sens, psi, quad_table, quad_index, counts, coords):
    def hbm(x):
        return pltpu.with_memory_space_constraint(x, pltpu.HBM)

    sens, coords = hbm(sens.transpose(1, 0, 2)), hbm(coords)
    small = hbm(counts), hbm(quad_table), hbm(quad_index.reshape(1, 256)), hbm(psi)
    keep, send, w, count_rows, *stream = first_part(*small, sens, coords)
    yield keep, send, w
    for part in range(1, counts.shape[0] // PART):
        keep, send, *stream = later_part(part, count_rows, w, stream, sens, coords)
        yield keep, send, w


def small_call(kernel, out_shape, in_specs, args, name, aliases=None):
    many = isinstance(out_shape, list)
    return pl.pallas_call(
        kernel,
        in_specs=in_specs,
        out_specs=[VMEM] * len(out_shape) if many else VMEM,
        out_shape=out_shape,
        input_output_aliases=aliases or {},
        cost_estimate=pl.CostEstimate(flops=1, bytes_accessed=1, transcendentals=0),
        compiler_params=pltpu.CompilerParams(vmem_limit_bytes=16 * MIB),
        name=name,
    )(*args)


def pair_sum_kernel(keep_ref, recv_ref, after_ref, sum_ref, send_ref):
    del after_ref
    total = keep_ref[...] + recv_ref[...].astype(jnp.float32)
    sum_ref[...] = total
    send_ref[...] = total.astype(jnp.bfloat16)


def pair_sum(keep, recv, after):
    out = [jax.ShapeDtypeStruct(keep.shape, t) for t in (jnp.float32, jnp.bfloat16)]
    in_specs = [VMEM, VMEM, pl.BlockSpec(memory_space=pl.ANY)]
    return small_call(pair_sum_kernel, out, in_specs, (keep, recv, after), "pair_sum")


def add_mine(cells_ref, start, dense_ref, tiles_ref):
    my_x, my_core = lax.axis_index("x"), lax.axis_index("core")
    for p in range(PART):
        cell = cells_ref[start + p]
        owner = lax.shift_right_logical(cell * 43691, 17)
        within = cell - 3 * owner

        @pl.when(((owner >> 5) == my_x) & ((owner & 1) == my_core))
        def _():
            at = ((owner & 31) >> 1) * 3 + within
            dense_ref[at] += tiles_ref[p].astype(jnp.float32)


SLOTS = (48, ROWS, LANES)
DENSE = jax.ShapeDtypeStruct(SLOTS, jnp.float32)


def add_kernel(plan, zero, last, *refs):
    cells, refs = refs[:2], refs[2:]
    tiles, refs = refs[: len(plan)], refs[len(plan) :]
    dense_ref = refs[0] if zero else refs[1]
    if zero:
        dense_ref[...] = jnp.zeros_like(dense_ref)
    for (which, part), ref in zip(plan, tiles):
        add_mine(cells[which], part * PART, dense_ref, ref)
    if last:
        refs[-1][...] = dense_ref[...].astype(jnp.bfloat16)


def add(cells, plan, tiles, dense=None, last=False):
    zero = dense is None
    args = [*cells, *tiles] + ([] if zero else [dense])
    specs = [SMEM] * 2 + [VMEM] * (len(args) - 2)
    out = [DENSE] + ([jax.ShapeDtypeStruct(SLOTS, jnp.bfloat16)] if last else [])
    aliases = {} if zero else {len(args) - 1: 0}
    return small_call(functools.partial(add_kernel, plan, zero, last), out, specs, args, "add", aliases)[-1]


def owner_sum_kernel(in_ref, out_ref):
    lower = lax.broadcasted_iota(jnp.int32, (ROWS, LANES), 1) < 64
    cell = []
    for e in range(3):
        total = in_ref[e].astype(jnp.float32)
        for j in range(1, in_ref.shape[0] // 3):
            total = total + in_ref[3 * j + e].astype(jnp.float32)
        cell.append(total)
    a, b, c = cell
    ab = jnp.concatenate([jnp.where(lower, a, pltpu.roll(b, 64, 1)), jnp.where(lower, pltpu.roll(a, 64, 1), b)], axis=0)
    cc = jnp.concatenate([c, pltpu.roll(c, 64, 1)], axis=0)
    out_ref[0:128, :] = ab.T[:, 0 : 3 * K]
    out_ref[128:192, :] = cc.T[0:64, 0 : 3 * K]


def double(step):
    near, far = (1, 0, 3, 2), (3, 2, 1, 0)
    order = (near, far) if step == 0 else (far, near)
    return [(2 * x + core, 2 * order[core][x] + core) for x in range(4) for core in range(2)]


def local(sens, psi, quad_table, quad_index, counts, cells, coords):
    swap = [(0, 1), (1, 0)]

    def smem(x):
        return pltpu.with_memory_space_constraint(x, pltpu.SMEM)

    other_cells = lax.ppermute(cells, "core", swap)
    held = []
    for keep, send, w in all_parts(sens, psi, quad_table, quad_index, counts, coords):
        held.append((keep, lax.ppermute(send, ("x", "core"), double(0))))
    after = w
    for i, (keep, recv) in enumerate(held):
        keep, after = pair_sum(keep, recv, after)
        held[i] = keep, lax.ppermute(after, ("x", "core"), double(1))
    both = smem(cells), smem(other_cells)
    count = len(held)
    full, swapped = [], []
    for i, (keep, recv) in enumerate(held):
        if i == count - 1:
            after = dense = add(both, [(0, j) for j in range(i)], full)
        tiles, after = pair_sum(keep, recv, after)
        full.append(tiles)
        swapped.append(lax.ppermute(after, "core", swap))
    plan = [(0, count - 1)] + [(1, j) for j in range(count - 1)]
    dense = add(both, plan, [full[-1]] + swapped[:-1], dense)
    slots = add(both, [(1, count - 1)], swapped[-1:], dense, True)
    slots = lax.all_to_all(slots, ("z", "y"), 0, 0, tiled=True)
    out = jax.ShapeDtypeStruct((192, 3 * K), jnp.float32)
    return small_call(owner_sum_kernel, out, [VMEM], (slots,), "owner_sum").T


def solution(mesh):
    inner = Mesh(mesh.devices.reshape(4, 4, 4, 2), ("x", "z", "y", "core"))
    surf = ("z", "y", "core")
    in_specs = (P("x", None, surf), P(), P(), P(), P(surf), P(surf), P(None, surf))
    out_specs = P(None, ("x",) + surf)
    return jax.shard_map(local, mesh=inner, in_specs=in_specs, out_specs=out_specs, check_vma=False)
```

```python
import functools

import jax
import jax.numpy as jnp
from jax import lax
from jax.experimental import pallas as pl
from jax.experimental.pallas import tpu as pltpu
from jax.sharding import Mesh, PartitionSpec as P

K = 35
NQW = 16
CELLS = 384
PATCH_PTS = 512
NODE_Q = 64
PART = 16
FIRST_CHUNKS = (4, 12)
NEXT_CHUNKS = (16,)
ROWS = 56
LANES = 128
MIB = 1 << 20
KERNEL_VMEM = 32 * MIB


def bernstein_rows(coords, count):
    shape = (8, PATCH_PTS)
    u, v, w = [jnp.broadcast_to(row, shape) for row in coords]
    sub = lax.broadcasted_iota(jnp.int32, shape, 0)
    lane = lax.broadcasted_iota(jnp.int32, shape, 1)
    live = (lane < count).astype(jnp.float32)

    def basis(a):
        one = 1.0 - a
        return one * one * one, 3.0 * a * one * one, 3.0 * a * a * one, a * a * a

    w0, w1, w2, w3 = basis(w)
    low = sub & 3
    wl = jnp.where(low == 0, w0, jnp.where(low == 1, w1, jnp.where(low == 2, w2, w3))) * live
    v0, v1, v2, v3 = basis(v)
    first = sub < 4
    pair01 = jnp.where(first, v0, v1) * wl
    pair23 = jnp.where(first, v2, v3) * wl
    rows = []
    for b in basis(u):
        rows += [b * pair01, b * pair23]
    return jnp.concatenate(rows, axis=0)


def split(x):
    high = x.astype(jnp.bfloat16)
    return high, (x - high.astype(jnp.float32)).astype(jnp.bfloat16)


SMEM = pl.BlockSpec(memory_space=pltpu.SMEM)
VMEM = pl.BlockSpec(memory_space=pltpu.VMEM)
HBM = pl.BlockSpec(memory_space=pltpu.HBM)


def weights(table_ref, index_ref, psi_ref, pad_ref, w_ref):
    index = index_ref[...]
    qweight = jnp.zeros(index.shape, jnp.float32)
    for j in range(NQW):
        qweight = jnp.where(index == j, table_ref[j], qweight)
    pad_ref[...] = jnp.zeros_like(pad_ref)
    pad_ref[0:K, :] = psi_ref[...] * qweight
    coef = pad_ref[...].astype(jnp.bfloat16)
    node = lax.axis_index("x")
    row = lax.broadcasted_iota(jnp.int32, (112, 40), 0)
    col = lax.broadcasted_iota(jnp.int32, (112, 40), 1)
    expand = ((row - 3 * col >= 0) & (row - 3 * col < 3)).astype(jnp.float32).astype(jnp.bfloat16)
    spread = jnp.dot(expand, coef, preferred_element_type=jnp.float32).astype(jnp.bfloat16)
    q = lax.broadcasted_iota(jnp.int32, (256, 192), 0)
    col = lax.broadcasted_iota(jnp.int32, (256, 192), 1)
    pick = (q == node * NODE_Q + (col & 63)).astype(jnp.float32).astype(jnp.bfloat16)
    full = jnp.dot(spread, pick, preferred_element_type=jnp.float32)
    row = lax.broadcasted_iota(jnp.int32, (112, 192), 0)
    col = lax.broadcasted_iota(jnp.int32, (112, 192), 1)
    w_ref[...] = jnp.where(row % 3 == col // 64, full, 0.0).astype(jnp.bfloat16)


def across(a, b):
    return lax.dot_general(a, b, (((1,), (1,)), ((), ())), preferred_element_type=jnp.float32)


def chunk_tiles(patches, counts, sens_ref, coords_ref, w, keep_ref, send_ref):
    lower = lax.broadcasted_iota(jnp.int32, (ROWS, LANES), 1) < 64
    for pair in range(patches.start, patches.stop, 2):
        sums = []
        for i in (pair, pair + 1):
            at = slice(i * PATCH_PTS, (i + 1) * PATCH_PTS)
            bern = bernstein_rows([coords_ref[c : c + 1, at] for c in range(3)], counts(i))
            basis = jnp.concatenate(split(bern), axis=0)
            s = across(basis, sens_ref[:, :, at].reshape(3 * NODE_Q, PATCH_PTS))
            sums.append(s[0:64] + s[64:128])
        high, low = split(jnp.concatenate(sums, axis=0))
        t = across(w, high) + across(w, low)
        top, bottom = t[0:ROWS], t[ROWS : 2 * ROWS]
        first = jnp.where(lower, top, pltpu.roll(bottom, 64, 1))
        second = jnp.where(lower, pltpu.roll(top, 64, 1), bottom)
        for i, x in ((pair, first), (pair + 1, second)):
            keep_ref[i] = x
            send_ref[i] = x.astype(jnp.bfloat16)


def chunks_of(sizes):
    ends = [sum(sizes[: i + 1]) for i in range(len(sizes))]
    return [range(end - size, end) for end, size in zip(ends, sizes)]


def part_copies(part, sizes, sens_hbm, coords_hbm, sens_buf, coords_buf, sem):
    copies = []
    for i, patches in enumerate(chunks_of(sizes)):
        count = len(patches) * PATCH_PTS
        here = pl.ds(patches.start * PATCH_PTS, count)
        there = pl.ds((part * PART + patches.start) * PATCH_PTS, count)
        copies.append(
            (
                pltpu.make_async_copy(sens_hbm.at[:, :, there], sens_buf.at[:, :, here], sem.at[i, 0]),
                pltpu.make_async_copy(coords_hbm.at[:, there], coords_buf.at[:, here], sem.at[i, 1]),
            )
        )
    return copies


def first_kernel(
    counts_hbm, table_hbm, index_hbm, psi_hbm, sens_hbm, coords_hbm,
    keep_ref, send_ref, w_ref, count_rows, sens_next, coords_next,
    sens_buf, coords_buf, sem, next_sem, counts_ref, table_ref, index_ref, psi_ref, small_sem, pad_ref
):
    pairs = ((table_hbm, table_ref), (index_hbm, index_ref), (psi_hbm, psi_ref), (counts_hbm, counts_ref))
    small = [pltpu.make_async_copy(a, b, small_sem.at[i]) for i, (a, b) in enumerate(pairs)]
    mine = part_copies(0, FIRST_CHUNKS, sens_hbm, coords_hbm, sens_buf, coords_buf, sem)
    later = part_copies(1, NEXT_CHUNKS, sens_hbm, coords_hbm, sens_next, coords_next, next_sem)
    for copy in [*mine[0], *small] + [c for pair in mine[1:] for c in pair]:
        copy.start()
    for copy in small:
        copy.wait()
    for p in range(count_rows.shape[0]):
        count_rows[p : p + 1, :] = jnp.full((1, LANES), counts_ref[p], jnp.int32)
    weights(table_ref, index_ref, psi_ref, pad_ref, w_ref)
    w = w_ref[...]
    for i, patches in enumerate(chunks_of(FIRST_CHUNKS)):
        for copy in mine[i]:
            copy.wait()
        for copy in later[i] if i < len(later) else ():
            copy.start()
        chunk_tiles(patches, lambda p: counts_ref[p], sens_buf, coords_buf, w, keep_ref, send_ref)
    for pair in later:
        for copy in pair:
            copy.wait()


def later_kernel(part, last, count_rows, w_ref, sens_buf, coords_buf, *rest):
    if last:
        keep_ref, send_ref = rest
        later = []
    else:
        sens_hbm, coords_hbm, keep_ref, send_ref, sens_next, coords_next, next_sem = rest
        later = part_copies(part + 1, NEXT_CHUNKS, sens_hbm, coords_hbm, sens_next, coords_next, next_sem)
    for pair in later:
        for copy in pair:
            copy.start()
    w = w_ref[...]

    def counts(p):
        row = count_rows[part * PART + p : part * PART + p + 1, :]
        return jnp.concatenate([row] * (PATCH_PTS // LANES), axis=1)

    chunk_tiles(range(PART), counts, sens_buf, coords_buf, w, keep_ref, send_ref)
    for pair in later:
        for copy in pair:
            copy.wait()


def kinds():
    return dict(
        compiler_params=pltpu.CompilerParams(vmem_limit_bytes=KERNEL_VMEM),
        cost_estimate=pl.CostEstimate(flops=int(8e9), bytes_accessed=int(4e6), transcendentals=0),
    )


TILES = [jax.ShapeDtypeStruct((PART, ROWS, LANES), t) for t in (jnp.float32, jnp.bfloat16)]
BUFFERS = ((3, NODE_Q, PART * PATCH_PTS), jnp.bfloat16), ((3, PART * PATCH_PTS), jnp.float32)
STREAM = [jax.ShapeDtypeStruct(*b) for b in BUFFERS]


def first_part(counts, table, index, psi, sens, coords):
    return pl.pallas_call(
        first_kernel,
        in_specs=[HBM] * 6,
        out_specs=[VMEM] * 6,
        out_shape=TILES
        + [jax.ShapeDtypeStruct((112, 192), jnp.bfloat16), jax.ShapeDtypeStruct((counts.shape[0], LANES), jnp.int32)]
        + STREAM,
        scratch_shapes=[pltpu.VMEM(*b) for b in BUFFERS]
        + [
            pltpu.SemaphoreType.DMA((len(FIRST_CHUNKS), 2)),
            pltpu.SemaphoreType.DMA((len(NEXT_CHUNKS), 2)),
            pltpu.SMEM(counts.shape, jnp.int32),
            pltpu.SMEM((NQW,), jnp.float32),
            pltpu.VMEM((1, 256), jnp.int32),
            pltpu.VMEM((K, 256), jnp.float32),
            pltpu.SemaphoreType.DMA((4,)),
            pltpu.VMEM((40, 256), jnp.float32),
        ],
        name="tiles_0",
        **kinds(),
    )(counts, table, index, psi, sens, coords)


def later_part(part, count_rows, w, stream, sens, coords):
    last = (part + 1) * PART * PATCH_PTS == sens.shape[2]
    return pl.pallas_call(
        functools.partial(later_kernel, part, last),
        in_specs=[VMEM] * 4 + ([] if last else [HBM] * 2),
        out_specs=[VMEM] * (2 if last else 4),
        out_shape=TILES + ([] if last else STREAM),
        scratch_shapes=[] if last else [pltpu.SemaphoreType.DMA((len(NEXT_CHUNKS), 2))],
        name="tiles_%d" % part,
        **kinds(),
    )(count_rows, w, *stream, *([] if last else [sens, coords]))


def all_parts(sens, psi, quad_table, quad_index, counts, coords):
    def hbm(x):
        return pltpu.with_memory_space_constraint(x, pltpu.HBM)

    sens, coords = hbm(sens.transpose(1, 0, 2)), hbm(coords)
    small = hbm(counts), hbm(quad_table), hbm(quad_index.reshape(1, 256)), hbm(psi)
    keep, send, w, count_rows, *stream = first_part(*small, sens, coords)
    yield keep, send, w
    for part in range(1, counts.shape[0] // PART):
        keep, send, *stream = later_part(part, count_rows, w, stream, sens, coords)
        yield keep, send, w


def small_call(kernel, out_shape, in_specs, args, name, aliases=None):
    many = isinstance(out_shape, list)
    return pl.pallas_call(
        kernel,
        in_specs=in_specs,
        out_specs=[VMEM] * len(out_shape) if many else VMEM,
        out_shape=out_shape,
        input_output_aliases=aliases or {},
        cost_estimate=pl.CostEstimate(flops=1, bytes_accessed=1, transcendentals=0),
        compiler_params=pltpu.CompilerParams(vmem_limit_bytes=16 * MIB),
        name=name,
    )(*args)


def pair_sum_kernel(keep_ref, recv_ref, after_ref, sum_ref, send_ref):
    del after_ref
    total = keep_ref[...] + recv_ref[...].astype(jnp.float32)
    sum_ref[...] = total
    send_ref[...] = total.astype(jnp.bfloat16)


def pair_sum(keep, recv, after):
    out = [jax.ShapeDtypeStruct(keep.shape, t) for t in (jnp.float32, jnp.bfloat16)]
    in_specs = [VMEM, VMEM, pl.BlockSpec(memory_space=pl.ANY)]
    return small_call(pair_sum_kernel, out, in_specs, (keep, recv, after), "pair_sum")


def add_mine(cells_ref, start, dense_ref, tiles_ref):
    my_x, my_core = lax.axis_index("x"), lax.axis_index("core")
    for p in range(PART):
        cell = cells_ref[start + p]
        owner = lax.shift_right_logical(cell * 43691, 17)
        within = cell - 3 * owner

        @pl.when(((owner >> 5) == my_x) & ((owner & 1) == my_core))
        def _():
            at = ((owner & 31) >> 1) * 3 + within
            dense_ref[at] += tiles_ref[p].astype(jnp.float32)


SLOTS = (48, ROWS, LANES)
DENSE = jax.ShapeDtypeStruct(SLOTS, jnp.float32)


def add_kernel(plan, zero, last, *refs):
    cells, refs = refs[:2], refs[2:]
    tiles, refs = refs[: len(plan)], refs[len(plan) :]
    dense_ref = refs[0] if zero else refs[1]
    if zero:
        dense_ref[...] = jnp.zeros_like(dense_ref)
    for (which, part), ref in zip(plan, tiles):
        add_mine(cells[which], part * PART, dense_ref, ref)
    if last:
        refs[-1][...] = dense_ref[...].astype(jnp.bfloat16)


def add(cells, plan, tiles, dense=None, last=False):
    zero = dense is None
    args = [*cells, *tiles] + ([] if zero else [dense])
    specs = [SMEM] * 2 + [VMEM] * (len(args) - 2)
    out = [DENSE] + ([jax.ShapeDtypeStruct(SLOTS, jnp.bfloat16)] if last else [])
    aliases = {} if zero else {len(args) - 1: 0}
    return small_call(functools.partial(add_kernel, plan, zero, last), out, specs, args, "add", aliases)[-1]


def owner_sum_kernel(in_ref, out_ref):
    lower = lax.broadcasted_iota(jnp.int32, (ROWS, LANES), 1) < 64
    cell = []
    for e in range(3):
        total = in_ref[e].astype(jnp.float32)
        for j in range(1, in_ref.shape[0] // 3):
            total = total + in_ref[3 * j + e].astype(jnp.float32)
        cell.append(total)
    a, b, c = cell
    ab = jnp.concatenate([jnp.where(lower, a, pltpu.roll(b, 64, 1)), jnp.where(lower, pltpu.roll(a, 64, 1), b)], axis=0)
    cc = jnp.concatenate([c, pltpu.roll(c, 64, 1)], axis=0)
    out_ref[0:128, :] = ab.T[:, 0 : 3 * K]
    out_ref[128:192, :] = cc.T[0:64, 0 : 3 * K]


def double(step):
    near, far = (1, 0, 3, 2), (3, 2, 1, 0)
    order = (near, far) if step == 0 else (far, near)
    return [(2 * x + core, 2 * order[core][x] + core) for x in range(4) for core in range(2)]


def local(sens, psi, quad_table, quad_index, counts, cells, coords):
    swap = [(0, 1), (1, 0)]

    def smem(x):
        return pltpu.with_memory_space_constraint(x, pltpu.SMEM)

    other_cells = lax.ppermute(cells, "core", swap)
    held = []
    for keep, send, w in all_parts(sens, psi, quad_table, quad_index, counts, coords):
        held.append((keep, lax.ppermute(send, ("x", "core"), double(len(held) % 2))))
    after = w
    for i, (keep, recv) in enumerate(held):
        keep, after = pair_sum(keep, recv, after)
        held[i] = keep, lax.ppermute(after, ("x", "core"), double((i + 1) % 2))
    both = smem(cells), smem(other_cells)
    count = len(held)
    full, swapped = [], []
    for i, (keep, recv) in enumerate(held):
        if i == count - 1:
            after = dense = add(both, [(0, j) for j in range(i)], full)
        tiles, after = pair_sum(keep, recv, after)
        full.append(tiles)
        swapped.append(lax.ppermute(after, "core", swap))
    plan = [(0, count - 1)] + [(1, j) for j in range(count - 1)]
    dense = add(both, plan, [full[-1]] + swapped[:-1], dense)
    slots = add(both, [(1, count - 1)], swapped[-1:], dense, True)
    slots = lax.all_to_all(slots, ("z", "y"), 0, 0, tiled=True)
    out = jax.ShapeDtypeStruct((192, 3 * K), jnp.float32)
    return small_call(owner_sum_kernel, out, [VMEM], (slots,), "owner_sum").T


def solution(mesh):
    inner = Mesh(mesh.devices.reshape(4, 4, 4, 2), ("x", "z", "y", "core"))
    surf = ("z", "y", "core")
    in_specs = (P("x", None, surf), P(), P(), P(), P(surf), P(surf), P(None, surf))
    out_specs = P(None, ("x",) + surf)
    return jax.shard_map(local, mesh=inner, in_specs=in_specs, out_specs=out_specs, check_vma=False)
```

```python
import functools

import jax
import jax.numpy as jnp
from jax import lax
from jax.experimental import pallas as pl
from jax.experimental.pallas import tpu as pltpu
from jax.sharding import Mesh, PartitionSpec as P

K = 35
NQW = 16
CELLS = 384
PATCH_PTS = 512
NODE_Q = 64
PART = 16
FIRST_CHUNKS = (4, 12)
NEXT_CHUNKS = (16,)
ROWS = 56
LANES = 128
MIB = 1 << 20
KERNEL_VMEM = 32 * MIB


def bernstein_rows(coords, count):
    shape = (8, PATCH_PTS)
    u, v, w = [jnp.broadcast_to(row, shape) for row in coords]
    sub = lax.broadcasted_iota(jnp.int32, shape, 0)
    lane = lax.broadcasted_iota(jnp.int32, shape, 1)
    live = (lane < count).astype(jnp.float32)

    def basis(a):
        one = 1.0 - a
        return one * one * one, 3.0 * a * one * one, 3.0 * a * a * one, a * a * a

    w0, w1, w2, w3 = basis(w)
    low = sub & 3
    wl = jnp.where(low == 0, w0, jnp.where(low == 1, w1, jnp.where(low == 2, w2, w3))) * live
    v0, v1, v2, v3 = basis(v)
    first = sub < 4
    pair01 = jnp.where(first, v0, v1) * wl
    pair23 = jnp.where(first, v2, v3) * wl
    rows = []
    for b in basis(u):
        rows += [b * pair01, b * pair23]
    return jnp.concatenate(rows, axis=0)


def split(x):
    high = x.astype(jnp.bfloat16)
    return high, (x - high.astype(jnp.float32)).astype(jnp.bfloat16)


SMEM = pl.BlockSpec(memory_space=pltpu.SMEM)
VMEM = pl.BlockSpec(memory_space=pltpu.VMEM)
HBM = pl.BlockSpec(memory_space=pltpu.HBM)


def weights(table_ref, index_ref, psi_ref, pad_ref, w_ref):
    index = index_ref[...]
    qweight = jnp.zeros(index.shape, jnp.float32)
    for j in range(NQW):
        qweight = jnp.where(index == j, table_ref[j], qweight)
    pad_ref[...] = jnp.zeros_like(pad_ref)
    pad_ref[0:K, :] = psi_ref[...] * qweight
    coef = pad_ref[...].astype(jnp.bfloat16)
    node = lax.axis_index("x")
    row = lax.broadcasted_iota(jnp.int32, (112, 40), 0)
    col = lax.broadcasted_iota(jnp.int32, (112, 40), 1)
    expand = ((row - 3 * col >= 0) & (row - 3 * col < 3)).astype(jnp.float32).astype(jnp.bfloat16)
    spread = jnp.dot(expand, coef, preferred_element_type=jnp.float32).astype(jnp.bfloat16)
    q = lax.broadcasted_iota(jnp.int32, (256, 192), 0)
    col = lax.broadcasted_iota(jnp.int32, (256, 192), 1)
    pick = (q == node * NODE_Q + (col & 63)).astype(jnp.float32).astype(jnp.bfloat16)
    full = jnp.dot(spread, pick, preferred_element_type=jnp.float32)
    row = lax.broadcasted_iota(jnp.int32, (112, 192), 0)
    col = lax.broadcasted_iota(jnp.int32, (112, 192), 1)
    w_ref[...] = jnp.where(row % 3 == col // 64, full, 0.0).astype(jnp.bfloat16)


def across(a, b):
    return lax.dot_general(a, b, (((1,), (1,)), ((), ())), preferred_element_type=jnp.float32)


def chunk_tiles(patches, counts, sens_ref, coords_ref, w, keep_ref, send_ref):
    lower = lax.broadcasted_iota(jnp.int32, (ROWS, LANES), 1) < 64
    for pair in range(patches.start, patches.stop, 2):
        sums = []
        for i in (pair, pair + 1):
            at = slice(i * PATCH_PTS, (i + 1) * PATCH_PTS)
            bern = bernstein_rows([coords_ref[c : c + 1, at] for c in range(3)], counts(i))
            basis = jnp.concatenate(split(bern), axis=0)
            s = across(basis, sens_ref[:, :, at].reshape(3 * NODE_Q, PATCH_PTS))
            sums.append(s[0:64] + s[64:128])
        high, low = split(jnp.concatenate(sums, axis=0))
        t = across(w, high) + across(w, low)
        top, bottom = t[0:ROWS], t[ROWS : 2 * ROWS]
        first = jnp.where(lower, top, pltpu.roll(bottom, 64, 1))
        second = jnp.where(lower, pltpu.roll(top, 64, 1), bottom)
        for i, x in ((pair, first), (pair + 1, second)):
            keep_ref[i] = x
            send_ref[i] = x.astype(jnp.bfloat16)


def chunks_of(sizes):
    ends = [sum(sizes[: i + 1]) for i in range(len(sizes))]
    return [range(end - size, end) for end, size in zip(ends, sizes)]


def part_copies(part, sizes, sens_hbm, coords_hbm, sens_buf, coords_buf, sem):
    copies = []
    for i, patches in enumerate(chunks_of(sizes)):
        count = len(patches) * PATCH_PTS
        here = pl.ds(patches.start * PATCH_PTS, count)
        there = pl.ds((part * PART + patches.start) * PATCH_PTS, count)
        copies.append(
            (
                pltpu.make_async_copy(sens_hbm.at[:, :, there], sens_buf.at[:, :, here], sem.at[i, 0]),
                pltpu.make_async_copy(coords_hbm.at[:, there], coords_buf.at[:, here], sem.at[i, 1]),
            )
        )
    return copies


def first_kernel(
    counts_hbm, table_hbm, index_hbm, psi_hbm, sens_hbm, coords_hbm,
    keep_ref, send_ref, w_ref, count_rows, sens_next, coords_next,
    sens_buf, coords_buf, sem, next_sem, counts_ref, table_ref, index_ref, psi_ref, small_sem, pad_ref
):
    pairs = ((table_hbm, table_ref), (index_hbm, index_ref), (psi_hbm, psi_ref), (counts_hbm, counts_ref))
    small = [pltpu.make_async_copy(a, b, small_sem.at[i]) for i, (a, b) in enumerate(pairs)]
    mine = part_copies(0, FIRST_CHUNKS, sens_hbm, coords_hbm, sens_buf, coords_buf, sem)
    later = part_copies(1, NEXT_CHUNKS, sens_hbm, coords_hbm, sens_next, coords_next, next_sem)
    for copy in [*mine[0], *small] + [c for pair in mine[1:] for c in pair]:
        copy.start()
    for copy in small:
        copy.wait()
    for copy in later[0]:
        copy.start()
    for p in range(count_rows.shape[0]):
        count_rows[p : p + 1, :] = jnp.full((1, LANES), counts_ref[p], jnp.int32)
    for copy in mine[0]:
        copy.wait()
    weights(table_ref, index_ref, psi_ref, pad_ref, w_ref)
    w = w_ref[...]
    for i, patches in enumerate(chunks_of(FIRST_CHUNKS)):
        for copy in mine[i] if i > 0 else ():
            copy.wait()
        chunk_tiles(patches, lambda p: counts_ref[p], sens_buf, coords_buf, w, keep_ref, send_ref)
    for pair in later:
        for copy in pair:
            copy.wait()


def later_kernel(part, last, count_rows, w_ref, sens_buf, coords_buf, *rest):
    if last:
        keep_ref, send_ref = rest
        later = []
    else:
        sens_hbm, coords_hbm, keep_ref, send_ref, sens_next, coords_next, next_sem = rest
        later = part_copies(part + 1, NEXT_CHUNKS, sens_hbm, coords_hbm, sens_next, coords_next, next_sem)
    for pair in later:
        for copy in pair:
            copy.start()
    w = w_ref[...]

    def counts(p):
        row = count_rows[part * PART + p : part * PART + p + 1, :]
        return jnp.concatenate([row] * (PATCH_PTS // LANES), axis=1)

    chunk_tiles(range(PART), counts, sens_buf, coords_buf, w, keep_ref, send_ref)
    for pair in later:
        for copy in pair:
            copy.wait()


def kinds():
    return dict(
        compiler_params=pltpu.CompilerParams(vmem_limit_bytes=KERNEL_VMEM),
        cost_estimate=pl.CostEstimate(flops=int(8e9), bytes_accessed=int(4e6), transcendentals=0),
    )


TILES = [jax.ShapeDtypeStruct((PART, ROWS, LANES), t) for t in (jnp.float32, jnp.bfloat16)]
BUFFERS = ((3, NODE_Q, PART * PATCH_PTS), jnp.bfloat16), ((3, PART * PATCH_PTS), jnp.float32)
STREAM = [jax.ShapeDtypeStruct(*b) for b in BUFFERS]


def first_part(counts, table, index, psi, sens, coords):
    return pl.pallas_call(
        first_kernel,
        in_specs=[HBM] * 6,
        out_specs=[VMEM] * 6,
        out_shape=TILES
        + [jax.ShapeDtypeStruct((112, 192), jnp.bfloat16), jax.ShapeDtypeStruct((counts.shape[0], LANES), jnp.int32)]
        + STREAM,
        scratch_shapes=[pltpu.VMEM(*b) for b in BUFFERS]
        + [
            pltpu.SemaphoreType.DMA((len(FIRST_CHUNKS), 2)),
            pltpu.SemaphoreType.DMA((len(NEXT_CHUNKS), 2)),
            pltpu.SMEM(counts.shape, jnp.int32),
            pltpu.SMEM((NQW,), jnp.float32),
            pltpu.VMEM((1, 256), jnp.int32),
            pltpu.VMEM((K, 256), jnp.float32),
            pltpu.SemaphoreType.DMA((4,)),
            pltpu.VMEM((40, 256), jnp.float32),
        ],
        name="tiles_0",
        **kinds(),
    )(counts, table, index, psi, sens, coords)


def later_part(part, count_rows, w, stream, sens, coords):
    last = (part + 1) * PART * PATCH_PTS == sens.shape[2]
    return pl.pallas_call(
        functools.partial(later_kernel, part, last),
        in_specs=[VMEM] * 4 + ([] if last else [HBM] * 2),
        out_specs=[VMEM] * (2 if last else 4),
        out_shape=TILES + ([] if last else STREAM),
        scratch_shapes=[] if last else [pltpu.SemaphoreType.DMA((len(NEXT_CHUNKS), 2))],
        name="tiles_%d" % part,
        **kinds(),
    )(count_rows, w, *stream, *([] if last else [sens, coords]))


def all_parts(sens, psi, quad_table, quad_index, counts, coords):
    def hbm(x):
        return pltpu.with_memory_space_constraint(x, pltpu.HBM)

    sens, coords = hbm(sens.transpose(1, 0, 2)), hbm(coords)
    small = hbm(counts), hbm(quad_table), hbm(quad_index.reshape(1, 256)), hbm(psi)
    keep, send, w, count_rows, *stream = first_part(*small, sens, coords)
    yield keep, send, w
    for part in range(1, counts.shape[0] // PART):
        keep, send, *stream = later_part(part, count_rows, w, stream, sens, coords)
        yield keep, send, w


def small_call(kernel, out_shape, in_specs, args, name, aliases=None):
    many = isinstance(out_shape, list)
    return pl.pallas_call(
        kernel,
        in_specs=in_specs,
        out_specs=[VMEM] * len(out_shape) if many else VMEM,
        out_shape=out_shape,
        input_output_aliases=aliases or {},
        cost_estimate=pl.CostEstimate(flops=1, bytes_accessed=1, transcendentals=0),
        compiler_params=pltpu.CompilerParams(vmem_limit_bytes=16 * MIB),
        name=name,
    )(*args)


def pair_sum_kernel(keep_ref, recv_ref, after_ref, sum_ref, send_ref):
    del after_ref
    total = keep_ref[...] + recv_ref[...].astype(jnp.float32)
    sum_ref[...] = total
    send_ref[...] = total.astype(jnp.bfloat16)


def pair_sum(keep, recv, after):
    out = [jax.ShapeDtypeStruct(keep.shape, t) for t in (jnp.float32, jnp.bfloat16)]
    in_specs = [VMEM, VMEM, pl.BlockSpec(memory_space=pl.ANY)]
    return small_call(pair_sum_kernel, out, in_specs, (keep, recv, after), "pair_sum")


def add_mine(cells_ref, start, dense_ref, tiles_ref):
    my_x, my_core = lax.axis_index("x"), lax.axis_index("core")
    for p in range(PART):
        cell = cells_ref[start + p]
        owner = lax.shift_right_logical(cell * 43691, 17)
        within = cell - 3 * owner

        @pl.when(((owner >> 5) == my_x) & ((owner & 1) == my_core))
        def _():
            at = (((owner >> 1) & 3) * 4 + ((owner >> 3) & 3)) * 3 + within
            dense_ref[at] += tiles_ref[p].astype(jnp.float32)


SLOTS = (48, ROWS, LANES)
DENSE = jax.ShapeDtypeStruct(SLOTS, jnp.float32)


def add_kernel(plan, zero, last, *refs):
    cells, refs = refs[:2], refs[2:]
    tiles, refs = refs[: len(plan)], refs[len(plan) :]
    dense_ref = refs[0] if zero else refs[1]
    if zero:
        dense_ref[...] = jnp.zeros_like(dense_ref)
    for (which, part), ref in zip(plan, tiles):
        add_mine(cells[which], part * PART, dense_ref, ref)
    if last:
        refs[-1][...] = dense_ref[...].astype(jnp.bfloat16)


def add(cells, plan, tiles, dense=None, last=False):
    zero = dense is None
    args = [*cells, *tiles] + ([] if zero else [dense])
    specs = [SMEM] * 2 + [VMEM] * (len(args) - 2)
    out = [DENSE] + ([jax.ShapeDtypeStruct(SLOTS, jnp.bfloat16)] if last else [])
    aliases = {} if zero else {len(args) - 1: 0}
    return small_call(functools.partial(add_kernel, plan, zero, last), out, specs, args, "add", aliases)[-1]


def owner_sum_kernel(in_ref, out_ref):
    lower = lax.broadcasted_iota(jnp.int32, (ROWS, LANES), 1) < 64
    cell = []
    for e in range(3):
        total = in_ref[e].astype(jnp.float32)
        for j in range(1, in_ref.shape[0] // 3):
            total = total + in_ref[3 * j + e].astype(jnp.float32)
        cell.append(total)
    a, b, c = cell
    ab = jnp.concatenate([jnp.where(lower, a, pltpu.roll(b, 64, 1)), jnp.where(lower, pltpu.roll(a, 64, 1), b)], axis=0)
    cc = jnp.concatenate([c, pltpu.roll(c, 64, 1)], axis=0)
    out_ref[0:128, :] = ab.T[:, 0 : 3 * K]
    out_ref[128:192, :] = cc.T[0:64, 0 : 3 * K]


def double(step):
    near, far = (1, 0, 3, 2), (3, 2, 1, 0)
    order = (near, far) if step == 0 else (far, near)
    return [(2 * x + core, 2 * order[core][x] + core) for x in range(4) for core in range(2)]


def local(sens, psi, quad_table, quad_index, counts, cells, coords):
    swap = [(0, 1), (1, 0)]

    def smem(x):
        return pltpu.with_memory_space_constraint(x, pltpu.SMEM)

    other_cells = lax.ppermute(cells, "core", swap)
    held = []
    for keep, send, w in all_parts(sens, psi, quad_table, quad_index, counts, coords):
        held.append((keep, lax.ppermute(send, ("x", "core"), double(len(held) % 2))))
    after = w
    for i, (keep, recv) in enumerate(held):
        keep, after = pair_sum(keep, recv, after)
        held[i] = keep, lax.ppermute(after, ("x", "core"), double((i + 1) % 2))
    both = smem(cells), smem(other_cells)
    count = len(held)
    full, swapped = [], []
    for i, (keep, recv) in enumerate(held):
        if i == count - 1:
            after = dense = add(both, [(0, j) for j in range(i)], full)
        tiles, after = pair_sum(keep, recv, after)
        full.append(tiles)
        swapped.append(lax.ppermute(after, "core", swap))
    plan = [(0, count - 1)] + [(1, j) for j in range(count - 1)]
    dense = add(both, plan, [full[-1]] + swapped[:-1], dense)
    slots = add(both, [(1, count - 1)], swapped[-1:], dense, True)
    slots = lax.all_to_all(slots, ("y", "z"), 0, 0, tiled=True)
    out = jax.ShapeDtypeStruct((192, 3 * K), jnp.float32)
    return small_call(owner_sum_kernel, out, [VMEM], (slots,), "owner_sum").T


def solution(mesh):
    inner = Mesh(mesh.devices.reshape(4, 4, 4, 2), ("x", "z", "y", "core"))
    surf = ("z", "y", "core")
    in_specs = (P("x", None, surf), P(), P(), P(), P(surf), P(surf), P(None, surf))
    out_specs = P(None, ("x",) + surf)
    return jax.shard_map(local, mesh=inner, in_specs=in_specs, out_specs=out_specs, check_vma=False)
```

```python
import functools

import jax
import jax.numpy as jnp
from jax import lax
from jax.experimental import pallas as pl
from jax.experimental.pallas import tpu as pltpu
from jax.sharding import Mesh, PartitionSpec as P

K = 35
NQW = 16
CELLS = 384
PATCH_PTS = 512
NODE_Q = 64
PART = 16
FIRST_CHUNKS = (4, 12)
NEXT_CHUNKS = (16,)
ROWS = 56
LANES = 128
MIB = 1 << 20
KERNEL_VMEM = 32 * MIB


def bernstein_rows(coords, count):
    shape = (8, PATCH_PTS)
    u, v, w = [jnp.broadcast_to(row, shape) for row in coords]
    sub = lax.broadcasted_iota(jnp.int32, shape, 0)
    lane = lax.broadcasted_iota(jnp.int32, shape, 1)
    live = (lane < count).astype(jnp.float32)

    def basis(a):
        one = 1.0 - a
        return one * one * one, 3.0 * a * one * one, 3.0 * a * a * one, a * a * a

    w0, w1, w2, w3 = basis(w)
    low = sub & 3
    wl = jnp.where(low == 0, w0, jnp.where(low == 1, w1, jnp.where(low == 2, w2, w3))) * live
    v0, v1, v2, v3 = basis(v)
    first = sub < 4
    pair01 = jnp.where(first, v0, v1) * wl
    pair23 = jnp.where(first, v2, v3) * wl
    rows = []
    for b in basis(u):
        rows += [b * pair01, b * pair23]
    return jnp.concatenate(rows, axis=0)


def split(x):
    high = x.astype(jnp.bfloat16)
    return high, (x - high.astype(jnp.float32)).astype(jnp.bfloat16)


SMEM = pl.BlockSpec(memory_space=pltpu.SMEM)
VMEM = pl.BlockSpec(memory_space=pltpu.VMEM)
HBM = pl.BlockSpec(memory_space=pltpu.HBM)


def weights(table_ref, index_ref, psi_ref, pad_ref, w_ref):
    index = index_ref[...]
    qweight = jnp.zeros(index.shape, jnp.float32)
    for j in range(NQW):
        qweight = jnp.where(index == j, table_ref[j], qweight)
    pad_ref[...] = jnp.zeros_like(pad_ref)
    pad_ref[0:K, :] = psi_ref[...] * qweight
    coef = pad_ref[...].astype(jnp.bfloat16)
    node = lax.axis_index("x")
    row = lax.broadcasted_iota(jnp.int32, (112, 40), 0)
    col = lax.broadcasted_iota(jnp.int32, (112, 40), 1)
    expand = ((row - 3 * col >= 0) & (row - 3 * col < 3)).astype(jnp.float32).astype(jnp.bfloat16)
    spread = jnp.dot(expand, coef, preferred_element_type=jnp.float32).astype(jnp.bfloat16)
    q = lax.broadcasted_iota(jnp.int32, (256, 192), 0)
    col = lax.broadcasted_iota(jnp.int32, (256, 192), 1)
    pick = (q == node * NODE_Q + (col & 63)).astype(jnp.float32).astype(jnp.bfloat16)
    full = jnp.dot(spread, pick, preferred_element_type=jnp.float32)
    row = lax.broadcasted_iota(jnp.int32, (112, 192), 0)
    col = lax.broadcasted_iota(jnp.int32, (112, 192), 1)
    w_ref[...] = jnp.where(row % 3 == col // 64, full, 0.0).astype(jnp.bfloat16)


def across(a, b):
    return lax.dot_general(a, b, (((1,), (1,)), ((), ())), preferred_element_type=jnp.float32)


def chunk_tiles(patches, counts, sens_ref, coords_ref, w, keep_ref, send_ref):
    lower = lax.broadcasted_iota(jnp.int32, (ROWS, LANES), 1) < 64
    for pair in range(patches.start, patches.stop, 2):
        sums = []
        for i in (pair, pair + 1):
            at = slice(i * PATCH_PTS, (i + 1) * PATCH_PTS)
            bern = bernstein_rows([coords_ref[c : c + 1, at] for c in range(3)], counts(i))
            basis = jnp.concatenate(split(bern), axis=0)
            s = across(basis, sens_ref[:, :, at].reshape(3 * NODE_Q, PATCH_PTS))
            sums.append(s[0:64] + s[64:128])
        high, low = split(jnp.concatenate(sums, axis=0))
        t = across(w, high) + across(w, low)
        top, bottom = t[0:ROWS], t[ROWS : 2 * ROWS]
        first = jnp.where(lower, top, pltpu.roll(bottom, 64, 1))
        second = jnp.where(lower, pltpu.roll(top, 64, 1), bottom)
        for i, x in ((pair, first), (pair + 1, second)):
            keep_ref[i] = x
            send_ref[i] = x.astype(jnp.bfloat16)


def chunks_of(sizes):
    ends = [sum(sizes[: i + 1]) for i in range(len(sizes))]
    return [range(end - size, end) for end, size in zip(ends, sizes)]


def part_copies(part, sizes, sens_hbm, coords_hbm, sens_buf, coords_buf, sem):
    copies = []
    for i, patches in enumerate(chunks_of(sizes)):
        count = len(patches) * PATCH_PTS
        here = pl.ds(patches.start * PATCH_PTS, count)
        there = pl.ds((part * PART + patches.start) * PATCH_PTS, count)
        copies.append(
            (
                pltpu.make_async_copy(sens_hbm.at[:, :, there], sens_buf.at[:, :, here], sem.at[i, 0]),
                pltpu.make_async_copy(coords_hbm.at[:, there], coords_buf.at[:, here], sem.at[i, 1]),
            )
        )
    return copies


def first_kernel(
    counts_hbm, table_hbm, index_hbm, psi_hbm, sens_hbm, coords_hbm,
    keep_ref, send_ref, w_ref, count_rows, sens_next, coords_next,
    sens_buf, coords_buf, sem, next_sem, counts_ref, table_ref, index_ref, psi_ref, small_sem, pad_ref
):
    pairs = ((table_hbm, table_ref), (index_hbm, index_ref), (psi_hbm, psi_ref), (counts_hbm, counts_ref))
    small = [pltpu.make_async_copy(a, b, small_sem.at[i]) for i, (a, b) in enumerate(pairs)]
    mine = part_copies(0, FIRST_CHUNKS, sens_hbm, coords_hbm, sens_buf, coords_buf, sem)
    later = part_copies(1, NEXT_CHUNKS, sens_hbm, coords_hbm, sens_next, coords_next, next_sem)
    for copy in [*mine[0], *small] + [c for pair in mine[1:] for c in pair]:
        copy.start()
    for copy in small:
        copy.wait()
    for copy in later[0]:
        copy.start()
    for p in range(count_rows.shape[0]):
        count_rows[p : p + 1, :] = jnp.full((1, LANES), counts_ref[p], jnp.int32)
    for copy in mine[0]:
        copy.wait()
    weights(table_ref, index_ref, psi_ref, pad_ref, w_ref)
    w = w_ref[...]
    for i, patches in enumerate(chunks_of(FIRST_CHUNKS)):
        for copy in mine[i] if i > 0 else ():
            copy.wait()
        chunk_tiles(patches, lambda p: counts_ref[p], sens_buf, coords_buf, w, keep_ref, send_ref)
    for pair in later:
        for copy in pair:
            copy.wait()


def later_kernel(part, last, count_rows, w_ref, sens_buf, coords_buf, *rest):
    if last:
        keep_ref, send_ref = rest
        later = []
    else:
        sens_hbm, coords_hbm, keep_ref, send_ref, sens_next, coords_next, next_sem = rest
        later = part_copies(part + 1, NEXT_CHUNKS, sens_hbm, coords_hbm, sens_next, coords_next, next_sem)
    for pair in later:
        for copy in pair:
            copy.start()
    w = w_ref[...]

    def counts(p):
        row = count_rows[part * PART + p : part * PART + p + 1, :]
        return jnp.concatenate([row] * (PATCH_PTS // LANES), axis=1)

    chunk_tiles(range(PART), counts, sens_buf, coords_buf, w, keep_ref, send_ref)
    for pair in later:
        for copy in pair:
            copy.wait()


def kinds():
    return dict(
        compiler_params=pltpu.CompilerParams(vmem_limit_bytes=KERNEL_VMEM),
        cost_estimate=pl.CostEstimate(flops=int(8e9), bytes_accessed=int(4e6), transcendentals=0),
    )


TILES = [jax.ShapeDtypeStruct((PART, ROWS, LANES), t) for t in (jnp.float32, jnp.bfloat16)]
BUFFERS = ((3, NODE_Q, PART * PATCH_PTS), jnp.bfloat16), ((3, PART * PATCH_PTS), jnp.float32)
STREAM = [jax.ShapeDtypeStruct(*b) for b in BUFFERS]


def first_part(counts, table, index, psi, sens, coords):
    return pl.pallas_call(
        first_kernel,
        in_specs=[HBM] * 6,
        out_specs=[VMEM] * 6,
        out_shape=TILES
        + [jax.ShapeDtypeStruct((112, 192), jnp.bfloat16), jax.ShapeDtypeStruct((counts.shape[0], LANES), jnp.int32)]
        + STREAM,
        scratch_shapes=[pltpu.VMEM(*b) for b in BUFFERS]
        + [
            pltpu.SemaphoreType.DMA((len(FIRST_CHUNKS), 2)),
            pltpu.SemaphoreType.DMA((len(NEXT_CHUNKS), 2)),
            pltpu.SMEM(counts.shape, jnp.int32),
            pltpu.SMEM((NQW,), jnp.float32),
            pltpu.VMEM((1, 256), jnp.int32),
            pltpu.VMEM((K, 256), jnp.float32),
            pltpu.SemaphoreType.DMA((4,)),
            pltpu.VMEM((40, 256), jnp.float32),
        ],
        name="tiles_0",
        **kinds(),
    )(counts, table, index, psi, sens, coords)


def later_part(part, count_rows, w, stream, sens, coords):
    last = (part + 1) * PART * PATCH_PTS == sens.shape[2]
    return pl.pallas_call(
        functools.partial(later_kernel, part, last),
        in_specs=[VMEM] * 4 + ([] if last else [HBM] * 2),
        out_specs=[VMEM] * (2 if last else 4),
        out_shape=TILES + ([] if last else STREAM),
        scratch_shapes=[] if last else [pltpu.SemaphoreType.DMA((len(NEXT_CHUNKS), 2))],
        name="tiles_%d" % part,
        **kinds(),
    )(count_rows, w, *stream, *([] if last else [sens, coords]))


def all_parts(sens, psi, quad_table, quad_index, counts, coords):
    def hbm(x):
        return pltpu.with_memory_space_constraint(x, pltpu.HBM)

    sens, coords = hbm(sens.transpose(1, 0, 2)), hbm(coords)
    small = hbm(counts), hbm(quad_table), hbm(quad_index.reshape(1, 256)), hbm(psi)
    keep, send, w, count_rows, *stream = first_part(*small, sens, coords)
    yield keep, send, w
    for part in range(1, counts.shape[0] // PART):
        keep, send, *stream = later_part(part, count_rows, w, stream, sens, coords)
        yield keep, send, w


def small_call(kernel, out_shape, in_specs, args, name, aliases=None):
    many = isinstance(out_shape, list)
    return pl.pallas_call(
        kernel,
        in_specs=in_specs,
        out_specs=[VMEM] * len(out_shape) if many else VMEM,
        out_shape=out_shape,
        input_output_aliases=aliases or {},
        cost_estimate=pl.CostEstimate(flops=1, bytes_accessed=1, transcendentals=0),
        compiler_params=pltpu.CompilerParams(vmem_limit_bytes=16 * MIB),
        name=name,
    )(*args)


def pair_sum_kernel(keep_ref, recv_ref, after_ref, sum_ref, send_ref):
    del after_ref
    total = keep_ref[...] + recv_ref[...].astype(jnp.float32)
    sum_ref[...] = total
    send_ref[...] = total.astype(jnp.bfloat16)


def pair_sum(keep, recv, after):
    out = [jax.ShapeDtypeStruct(keep.shape, t) for t in (jnp.float32, jnp.bfloat16)]
    in_specs = [VMEM, VMEM, pl.BlockSpec(memory_space=pl.ANY)]
    return small_call(pair_sum_kernel, out, in_specs, (keep, recv, after), "pair_sum")


def add_mine(cells_ref, start, dense_ref, tiles_ref):
    my_x, my_core = lax.axis_index("x"), lax.axis_index("core")
    for p in range(PART):
        cell = cells_ref[start + p]
        owner = lax.shift_right_logical(cell * 43691, 17)
        within = cell - 3 * owner

        @pl.when(((owner >> 5) == my_x) & ((owner & 1) == my_core))
        def _():
            at = (((owner >> 1) & 3) * 4 + ((owner >> 3) & 3)) * 3 + within
            dense_ref[at] += tiles_ref[p].astype(jnp.float32)


SLOTS = (48, ROWS, LANES)
DENSE = jax.ShapeDtypeStruct(SLOTS, jnp.float32)


def add_kernel(plan, zero, last, *refs):
    cells, refs = refs[:2], refs[2:]
    tiles, refs = refs[: len(plan)], refs[len(plan) :]
    dense_ref = refs[0] if zero else refs[1]
    if zero:
        dense_ref[...] = jnp.zeros_like(dense_ref)
    for (which, part), ref in zip(plan, tiles):
        add_mine(cells[which], part * PART, dense_ref, ref)
    if last:
        refs[-1][...] = dense_ref[...].astype(jnp.bfloat16)


def add(cells, plan, tiles, dense=None, last=False):
    zero = dense is None
    args = [*cells, *tiles] + ([] if zero else [dense])
    specs = [SMEM] * 2 + [VMEM] * (len(args) - 2)
    out = [DENSE] + ([jax.ShapeDtypeStruct(SLOTS, jnp.bfloat16)] if last else [])
    aliases = {} if zero else {len(args) - 1: 0}
    return small_call(functools.partial(add_kernel, plan, zero, last), out, specs, args, "add", aliases)[-1]


def owner_sum_kernel(in_ref, out_ref):
    lower = lax.broadcasted_iota(jnp.int32, (ROWS, LANES), 1) < 64
    cell = []
    for e in range(3):
        total = in_ref[e].astype(jnp.float32)
        for j in range(1, in_ref.shape[0] // 3):
            total = total + in_ref[3 * j + e].astype(jnp.float32)
        cell.append(total)
    a, b, c = cell
    ab = jnp.concatenate([jnp.where(lower, a, pltpu.roll(b, 64, 1)), jnp.where(lower, pltpu.roll(a, 64, 1), b)], axis=0)
    cc = jnp.concatenate([c, pltpu.roll(c, 64, 1)], axis=0)
    out_ref[0:128, :] = ab.T[:, 0 : 3 * K]
    out_ref[128:192, :] = cc.T[0:64, 0 : 3 * K]


def double(step):
    near, far = (1, 0, 3, 2), (3, 2, 1, 0)
    order = (near, far) if step == 0 else (far, near)
    return [(2 * x + core, 2 * order[core][x] + core) for x in range(4) for core in range(2)]


def local(sens, psi, quad_table, quad_index, counts, cells, coords):
    swap = [(0, 1), (1, 0)]

    def smem(x):
        return pltpu.with_memory_space_constraint(x, pltpu.SMEM)

    other_cells = lax.ppermute(cells, "core", swap)
    held = []
    for keep, send, w in all_parts(sens, psi, quad_table, quad_index, counts, coords):
        held.append((keep, lax.ppermute(send, ("x", "core"), double(len(held) % 2))))
    after = other_cells
    for i, (keep, recv) in enumerate(held):
        keep, after = pair_sum(keep, recv, after)
        held[i] = keep, lax.ppermute(after, ("x", "core"), double((i + 1) % 2))
    both = smem(cells), smem(other_cells)
    count = len(held)
    full, swapped = [], []
    for i, (keep, recv) in enumerate(held):
        tiles, after = pair_sum(keep, recv, after)
        full.append(tiles)
        swapped.append(lax.ppermute(after, "core", swap))
    plan = [(0, j) for j in range(count)] + [(1, j) for j in range(count - 1)]
    dense = add(both, plan, full + swapped[:-1])
    slots = add(both, [(1, count - 1)], swapped[-1:], dense, True)
    slots = lax.all_to_all(slots, ("y", "z"), 0, 0, tiled=True)
    out = jax.ShapeDtypeStruct((192, 3 * K), jnp.float32)
    return small_call(owner_sum_kernel, out, [VMEM], (slots,), "owner_sum").T


def solution(mesh):
    inner = Mesh(mesh.devices.reshape(4, 4, 4, 2), ("x", "z", "y", "core"))
    surf = ("z", "y", "core")
    in_specs = (P("x", None, surf), P(), P(), P(), P(surf), P(surf), P(None, surf))
    out_specs = P(None, ("x",) + surf)
    return jax.shard_map(local, mesh=inner, in_specs=in_specs, out_specs=out_specs, check_vma=False)
```

```python
import functools

import jax
import jax.numpy as jnp
from jax import lax
from jax.experimental import pallas as pl
from jax.experimental.pallas import tpu as pltpu
from jax.sharding import Mesh, PartitionSpec as P

K = 35
NQW = 16
CELLS = 384
PATCH_PTS = 512
NODE_Q = 64
PART = 16
FIRST_CHUNKS = (2, 14)
NEXT_CHUNKS = (16,)
ROWS = 56
LANES = 128
MIB = 1 << 20
KERNEL_VMEM = 32 * MIB


def bernstein_rows(coords, count):
    shape = (8, PATCH_PTS)
    u, v, w = [jnp.broadcast_to(row, shape) for row in coords]
    sub = lax.broadcasted_iota(jnp.int32, shape, 0)
    lane = lax.broadcasted_iota(jnp.int32, shape, 1)
    live = (lane < count).astype(jnp.float32)

    def basis(a):
        one = 1.0 - a
        return one * one * one, 3.0 * a * one * one, 3.0 * a * a * one, a * a * a

    w0, w1, w2, w3 = basis(w)
    low = sub & 3
    wl = jnp.where(low == 0, w0, jnp.where(low == 1, w1, jnp.where(low == 2, w2, w3))) * live
    v0, v1, v2, v3 = basis(v)
    first = sub < 4
    pair01 = jnp.where(first, v0, v1) * wl
    pair23 = jnp.where(first, v2, v3) * wl
    rows = []
    for b in basis(u):
        rows += [b * pair01, b * pair23]
    return jnp.concatenate(rows, axis=0)


def split(x):
    high = x.astype(jnp.bfloat16)
    return high, (x - high.astype(jnp.float32)).astype(jnp.bfloat16)


SMEM = pl.BlockSpec(memory_space=pltpu.SMEM)
VMEM = pl.BlockSpec(memory_space=pltpu.VMEM)
HBM = pl.BlockSpec(memory_space=pltpu.HBM)


def weights(table_ref, index_ref, psi_ref, pad_ref, w_ref):
    index = index_ref[...]
    qweight = jnp.zeros(index.shape, jnp.float32)
    for j in range(NQW):
        qweight = jnp.where(index == j, table_ref[j], qweight)
    pad_ref[...] = jnp.zeros_like(pad_ref)
    pad_ref[0:K, :] = psi_ref[...] * qweight
    coef = pad_ref[...].astype(jnp.bfloat16)
    node = lax.axis_index("x")
    row = lax.broadcasted_iota(jnp.int32, (112, 40), 0)
    col = lax.broadcasted_iota(jnp.int32, (112, 40), 1)
    expand = ((row - 3 * col >= 0) & (row - 3 * col < 3)).astype(jnp.float32).astype(jnp.bfloat16)
    spread = jnp.dot(expand, coef, preferred_element_type=jnp.float32).astype(jnp.bfloat16)
    q = lax.broadcasted_iota(jnp.int32, (256, 192), 0)
    col = lax.broadcasted_iota(jnp.int32, (256, 192), 1)
    pick = (q == node * NODE_Q + (col & 63)).astype(jnp.float32).astype(jnp.bfloat16)
    full = jnp.dot(spread, pick, preferred_element_type=jnp.float32)
    row = lax.broadcasted_iota(jnp.int32, (112, 192), 0)
    col = lax.broadcasted_iota(jnp.int32, (112, 192), 1)
    w_ref[...] = jnp.where(row % 3 == col // 64, full, 0.0).astype(jnp.bfloat16)


def across(a, b):
    return lax.dot_general(a, b, (((1,), (1,)), ((), ())), preferred_element_type=jnp.float32)


def chunk_tiles(patches, counts, sens_ref, coords_ref, w, keep_ref, send_ref):
    lower = lax.broadcasted_iota(jnp.int32, (ROWS, LANES), 1) < 64
    for pair in range(patches.start, patches.stop, 2):
        sums = []
        for i in (pair, pair + 1):
            at = slice(i * PATCH_PTS, (i + 1) * PATCH_PTS)
            bern = bernstein_rows([coords_ref[c : c + 1, at] for c in range(3)], counts(i))
            basis = jnp.concatenate(split(bern), axis=0)
            s = across(basis, sens_ref[:, :, at].reshape(3 * NODE_Q, PATCH_PTS))
            sums.append(s[0:64] + s[64:128])
        high, low = split(jnp.concatenate(sums, axis=0))
        t = across(w, high) + across(w, low)
        top, bottom = t[0:ROWS], t[ROWS : 2 * ROWS]
        first = jnp.where(lower, top, pltpu.roll(bottom, 64, 1))
        second = jnp.where(lower, pltpu.roll(top, 64, 1), bottom)
        for i, x in ((pair, first), (pair + 1, second)):
            keep_ref[i] = x
            send_ref[i] = x.astype(jnp.bfloat16)


def chunks_of(sizes):
    ends = [sum(sizes[: i + 1]) for i in range(len(sizes))]
    return [range(end - size, end) for end, size in zip(ends, sizes)]


def part_copies(part, sizes, sens_hbm, coords_hbm, sens_buf, coords_buf, sem):
    copies = []
    for i, patches in enumerate(chunks_of(sizes)):
        count = len(patches) * PATCH_PTS
        here = pl.ds(patches.start * PATCH_PTS, count)
        there = pl.ds((part * PART + patches.start) * PATCH_PTS, count)
        copies.append(
            (
                pltpu.make_async_copy(sens_hbm.at[:, :, there], sens_buf.at[:, :, here], sem.at[i, 0]),
                pltpu.make_async_copy(coords_hbm.at[:, there], coords_buf.at[:, here], sem.at[i, 1]),
            )
        )
    return copies


def first_kernel(
    counts_hbm, table_hbm, index_hbm, psi_hbm, sens_hbm, coords_hbm,
    keep_ref, send_ref, w_ref, count_rows, sens_next, coords_next,
    sens_buf, coords_buf, sem, next_sem, counts_ref, table_ref, index_ref, psi_ref, small_sem, pad_ref
):
    pairs = ((table_hbm, table_ref), (index_hbm, index_ref), (psi_hbm, psi_ref), (counts_hbm, counts_ref))
    small = [pltpu.make_async_copy(a, b, small_sem.at[i]) for i, (a, b) in enumerate(pairs)]
    mine = part_copies(0, FIRST_CHUNKS, sens_hbm, coords_hbm, sens_buf, coords_buf, sem)
    later = part_copies(1, NEXT_CHUNKS, sens_hbm, coords_hbm, sens_next, coords_next, next_sem)
    for copy in [*mine[0], *small] + [c for pair in mine[1:] for c in pair]:
        copy.start()
    for copy in small:
        copy.wait()
    for copy in later[0]:
        copy.start()
    for p in range(count_rows.shape[0]):
        count_rows[p : p + 1, :] = jnp.full((1, LANES), counts_ref[p], jnp.int32)
    for copy in mine[0]:
        copy.wait()
    weights(table_ref, index_ref, psi_ref, pad_ref, w_ref)
    w = w_ref[...]
    for i, patches in enumerate(chunks_of(FIRST_CHUNKS)):
        for copy in mine[i] if i > 0 else ():
            copy.wait()
        chunk_tiles(patches, lambda p: counts_ref[p], sens_buf, coords_buf, w, keep_ref, send_ref)
    for pair in later:
        for copy in pair:
            copy.wait()


def later_kernel(part, last, count_rows, w_ref, sens_buf, coords_buf, *rest):
    if last:
        keep_ref, send_ref = rest
        later = []
    else:
        sens_hbm, coords_hbm, keep_ref, send_ref, sens_next, coords_next, next_sem = rest
        later = part_copies(part + 1, NEXT_CHUNKS, sens_hbm, coords_hbm, sens_next, coords_next, next_sem)
    for pair in later:
        for copy in pair:
            copy.start()
    w = w_ref[...]

    def counts(p):
        row = count_rows[part * PART + p : part * PART + p + 1, :]
        return jnp.concatenate([row] * (PATCH_PTS // LANES), axis=1)

    chunk_tiles(range(PART), counts, sens_buf, coords_buf, w, keep_ref, send_ref)
    for pair in later:
        for copy in pair:
            copy.wait()


def kinds():
    return dict(
        compiler_params=pltpu.CompilerParams(vmem_limit_bytes=KERNEL_VMEM),
        cost_estimate=pl.CostEstimate(flops=int(8e9), bytes_accessed=int(4e6), transcendentals=0),
    )


TILES = [jax.ShapeDtypeStruct((PART, ROWS, LANES), t) for t in (jnp.float32, jnp.bfloat16)]
BUFFERS = ((3, NODE_Q, PART * PATCH_PTS), jnp.bfloat16), ((3, PART * PATCH_PTS), jnp.float32)
STREAM = [jax.ShapeDtypeStruct(*b) for b in BUFFERS]


def first_part(counts, table, index, psi, sens, coords):
    return pl.pallas_call(
        first_kernel,
        in_specs=[HBM] * 6,
        out_specs=[VMEM] * 6,
        out_shape=TILES
        + [jax.ShapeDtypeStruct((112, 192), jnp.bfloat16), jax.ShapeDtypeStruct((counts.shape[0], LANES), jnp.int32)]
        + STREAM,
        scratch_shapes=[pltpu.VMEM(*b) for b in BUFFERS]
        + [
            pltpu.SemaphoreType.DMA((len(FIRST_CHUNKS), 2)),
            pltpu.SemaphoreType.DMA((len(NEXT_CHUNKS), 2)),
            pltpu.SMEM(counts.shape, jnp.int32),
            pltpu.SMEM((NQW,), jnp.float32),
            pltpu.VMEM((1, 256), jnp.int32),
            pltpu.VMEM((K, 256), jnp.float32),
            pltpu.SemaphoreType.DMA((4,)),
            pltpu.VMEM((40, 256), jnp.float32),
        ],
        name="tiles_0",
        **kinds(),
    )(counts, table, index, psi, sens, coords)


def later_part(part, count_rows, w, stream, sens, coords):
    last = (part + 1) * PART * PATCH_PTS == sens.shape[2]
    return pl.pallas_call(
        functools.partial(later_kernel, part, last),
        in_specs=[VMEM] * 4 + ([] if last else [HBM] * 2),
        out_specs=[VMEM] * (2 if last else 4),
        out_shape=TILES + ([] if last else STREAM),
        scratch_shapes=[] if last else [pltpu.SemaphoreType.DMA((len(NEXT_CHUNKS), 2))],
        name="tiles_%d" % part,
        **kinds(),
    )(count_rows, w, *stream, *([] if last else [sens, coords]))


def all_parts(sens, psi, quad_table, quad_index, counts, coords):
    def hbm(x):
        return pltpu.with_memory_space_constraint(x, pltpu.HBM)

    sens, coords = hbm(sens.transpose(1, 0, 2)), hbm(coords)
    small = hbm(counts), hbm(quad_table), hbm(quad_index.reshape(1, 256)), hbm(psi)
    keep, send, w, count_rows, *stream = first_part(*small, sens, coords)
    yield keep, send, w
    for part in range(1, counts.shape[0] // PART):
        keep, send, *stream = later_part(part, count_rows, w, stream, sens, coords)
        yield keep, send, w


def small_call(kernel, out_shape, in_specs, args, name, aliases=None):
    many = isinstance(out_shape, list)
    return pl.pallas_call(
        kernel,
        in_specs=in_specs,
        out_specs=[VMEM] * len(out_shape) if many else VMEM,
        out_shape=out_shape,
        input_output_aliases=aliases or {},
        cost_estimate=pl.CostEstimate(flops=1, bytes_accessed=1, transcendentals=0),
        compiler_params=pltpu.CompilerParams(vmem_limit_bytes=16 * MIB),
        name=name,
    )(*args)


def pair_sum_kernel(keep_ref, recv_ref, after_ref, sum_ref, send_ref):
    del after_ref
    total = keep_ref[...] + recv_ref[...].astype(jnp.float32)
    sum_ref[...] = total
    send_ref[...] = total.astype(jnp.bfloat16)


def pair_sum(keep, recv, after):
    out = [jax.ShapeDtypeStruct(keep.shape, t) for t in (jnp.float32, jnp.bfloat16)]
    in_specs = [VMEM, VMEM, pl.BlockSpec(memory_space=pl.ANY)]
    return small_call(pair_sum_kernel, out, in_specs, (keep, recv, after), "pair_sum")


def add_mine(cells_ref, start, dense_ref, tiles_ref):
    my_x, my_core = lax.axis_index("x"), lax.axis_index("core")
    for p in range(PART):
        cell = cells_ref[start + p]
        owner = lax.shift_right_logical(cell * 43691, 17)
        within = cell - 3 * owner

        @pl.when(((owner >> 5) == my_x) & ((owner & 1) == my_core))
        def _():
            at = (((owner >> 1) & 3) * 4 + ((owner >> 3) & 3)) * 3 + within
            dense_ref[at] += tiles_ref[p].astype(jnp.float32)


SLOTS = (48, ROWS, LANES)
DENSE = jax.ShapeDtypeStruct(SLOTS, jnp.float32)


def add_kernel(plan, zero, last, *refs):
    cells, refs = refs[:2], refs[2:]
    tiles, refs = refs[: len(plan)], refs[len(plan) :]
    dense_ref = refs[0] if zero else refs[1]
    if zero:
        dense_ref[...] = jnp.zeros_like(dense_ref)
    for (which, part), ref in zip(plan, tiles):
        add_mine(cells[which], part * PART, dense_ref, ref)
    if last:
        refs[-1][...] = dense_ref[...].astype(jnp.bfloat16)


def add(cells, plan, tiles, dense=None, last=False):
    zero = dense is None
    args = [*cells, *tiles] + ([] if zero else [dense])
    specs = [SMEM] * 2 + [VMEM] * (len(args) - 2)
    out = [DENSE] + ([jax.ShapeDtypeStruct(SLOTS, jnp.bfloat16)] if last else [])
    aliases = {} if zero else {len(args) - 1: 0}
    return small_call(functools.partial(add_kernel, plan, zero, last), out, specs, args, "add", aliases)[-1]


def owner_sum_kernel(in_ref, out_ref):
    lower = lax.broadcasted_iota(jnp.int32, (ROWS, LANES), 1) < 64
    cell = []
    for e in range(3):
        total = in_ref[e].astype(jnp.float32)
        for j in range(1, in_ref.shape[0] // 3):
            total = total + in_ref[3 * j + e].astype(jnp.float32)
        cell.append(total)
    a, b, c = cell
    ab = jnp.concatenate([jnp.where(lower, a, pltpu.roll(b, 64, 1)), jnp.where(lower, pltpu.roll(a, 64, 1), b)], axis=0)
    cc = jnp.concatenate([c, pltpu.roll(c, 64, 1)], axis=0)
    out_ref[0:128, :] = ab.T[:, 0 : 3 * K]
    out_ref[128:192, :] = cc.T[0:64, 0 : 3 * K]


def double(step):
    near, far = (1, 0, 3, 2), (3, 2, 1, 0)
    order = (near, far) if step == 0 else (far, near)
    return [(2 * x + core, 2 * order[core][x] + core) for x in range(4) for core in range(2)]


def local(sens, psi, quad_table, quad_index, counts, cells, coords):
    swap = [(0, 1), (1, 0)]

    def smem(x):
        return pltpu.with_memory_space_constraint(x, pltpu.SMEM)

    other_cells = lax.ppermute(cells, "core", swap)
    held = []
    for keep, send, w in all_parts(sens, psi, quad_table, quad_index, counts, coords):
        held.append((keep, lax.ppermute(send, ("x", "core"), double(len(held) % 2))))
    after = other_cells
    for i, (keep, recv) in enumerate(held):
        keep, after = pair_sum(keep, recv, after)
        held[i] = keep, lax.ppermute(after, ("x", "core"), double((i + 1) % 2))
    both = smem(cells), smem(other_cells)
    count = len(held)
    full, swapped = [], []
    for i, (keep, recv) in enumerate(held):
        tiles, after = pair_sum(keep, recv, after)
        full.append(tiles)
        swapped.append(lax.ppermute(after, "core", swap))
    plan = [(0, j) for j in range(count)] + [(1, j) for j in range(count - 1)]
    dense = add(both, plan, full + swapped[:-1])
    slots = add(both, [(1, count - 1)], swapped[-1:], dense, True)
    slots = lax.all_to_all(slots, ("y", "z"), 0, 0, tiled=True)
    out = jax.ShapeDtypeStruct((192, 3 * K), jnp.float32)
    return small_call(owner_sum_kernel, out, [VMEM], (slots,), "owner_sum").T


def solution(mesh):
    inner = Mesh(mesh.devices.reshape(4, 4, 4, 2), ("x", "z", "y", "core"))
    surf = ("z", "y", "core")
    in_specs = (P("x", None, surf), P(), P(), P(), P(surf), P(surf), P(None, surf))
    out_specs = P(None, ("x",) + surf)
    return jax.shard_map(local, mesh=inner, in_specs=in_specs, out_specs=out_specs, check_vma=False)
```
